128 devices in a mesh: pair: 4 (over y), db: 32 (over x, z, core).
Axes of the slice: x: 4, y: 4, z: 4, core: 2. Of those that a mesh axis runs over, the one named last changes fastest.
Arguments:
- forward_strain: bfloat16 [4, 2048, 6, 8192], P('pair', 'db'), may hold values from -6 to 6
- backward_strain: bfloat16 [4, 2048, 6, 8192], P('pair', 'db'), may hold values from -6 to 6
- request_point: int32 [32, 32, 8], P('db'), may hold values from 0 to 63
- node_slot: int32 [2, 8, 16384], P(None, None, 'db'), may hold values from 0 to 255, as said below
- node_weight: float32 [2, 8, 16384], P(None, None, 'db'), may hold values from 0.05 to 0.25
- band_filter: float32 [16, 512], replicated, may hold values from 0.1 to 1
- misfit: float32 [32, 16], replicated, may hold values from 0.1 to 1
- pair_group: int32 [32], replicated, may hold values from 0 to 3, as said below
Outputs:
- kernel: float32 [16, 16384], P('pair', 'db')
The draws below stay inside these ranges and needn't reach their ends.
Inputs may be any that keep to these rules, and one draw needn't show every extreme that they name: For each w, all 8 nodes of one inversion point come from one database device; the forward device and the backward device of a point always differ. node_slot = d * 8 + c, where c is below the number of slots that d fills for the point's owner, which is 1 to 8. The last database device fills 8 slots for every owner, and one owner receives 8 slots from every database device. Slots that no node names may hold any local point. `pair_group`: each group holds exactly 8 station pairs.
All inputs are finite; a program needn't handle non-finite values.
Results may differ from the reference program's by a relative error of at most 0.0052.
Values may be sent and summed in bfloat16 or wider, within the bound.
A program may use at most 128 MiB of HBM per device.

```python
import math
import jax
import jax.numpy as jnp
from jax import lax

NT = 8192
NF = 512
BANDS = 16
COMPS = 6
K = 8
CAP = 8
PDB_DEV = 64
POINTS_DEV = 512
GROUPS = 4
OWNERS = 32
NDB = 2048
POINTS = 16384
STATION_PAIRS = 32


def draw_node_slot(key, part):
    key = jax.random.fold_in(key, 11)
    subkeys = jax.random.split(key, 7)
    counts = jax.random.randint(subkeys[0], (OWNERS, OWNERS), 1, CAP + 1)
    busy_owner = jax.random.randint(subkeys[1], (), 0, OWNERS)
    owner_range = jnp.arange(OWNERS)
    counts = jnp.where(owner_range[None, :] == busy_owner, CAP, counts)
    counts = jnp.where(owner_range[:, None] == OWNERS - 1, CAP, counts)
    point_range = jnp.arange(POINTS)
    owner_index = point_range // POINTS_DEV
    forced_local = jax.random.randint(subkeys[2], (OWNERS,), 0, POINTS_DEV)
    forced = point_range % POINTS_DEV == forced_local[owner_index]
    source = jax.random.randint(subkeys[3], (POINTS,), 0, OWNERS)
    source = jnp.where(forced, OWNERS - 1, source)
    offset = jax.random.randint(subkeys[5], (POINTS,), 1, OWNERS)
    other = (source + offset) % OWNERS
    first_node = jnp.arange(K)[:, None] == 0
    limit_fwd = counts[source, owner_index]
    raw_fwd = jax.random.randint(subkeys[4], (K, POINTS), 0, 1 << 20)
    picks_fwd = raw_fwd % limit_fwd[None, :]
    picks_fwd = jnp.where(first_node & forced[None, :], CAP - 1, picks_fwd)
    limit_bwd = counts[other, owner_index]
    raw_bwd = jax.random.randint(subkeys[6], (K, POINTS), 0, 1 << 20)
    picks_bwd = raw_bwd % limit_bwd[None, :]
    slot_fwd = source[None, :] * CAP + picks_fwd
    slot_bwd = other[None, :] * CAP + picks_bwd
    return jnp.stack([slot_fwd, slot_bwd], axis=0).astype(jnp.int32)


def draw_pair_group(key, part):
    key = jax.random.fold_in(key, 23)
    order = jax.random.permutation(key, STATION_PAIRS)
    return (order % GROUPS).astype(jnp.int32)


def with_ends(drawn, own_key, least, top_value):
    longest = drawn.shape.index(max(drawn.shape))
    spots = []
    for shift in (0, 1):
        where = [jax.random.randint(jax.random.fold_in(own_key, axis), (), 0, length) for axis, length in enumerate(drawn.shape)]
        where[longest] = (where[longest] + shift) % drawn.shape[longest]
        spots.append(tuple(where))
    return drawn.at[spots[0]].set(least).at[spots[1]].set(top_value)


def levels(own_key, dims, cuts, least, largest):
    factor_of = 1.0
    for dim, parts in cuts:
        heights = jax.random.uniform(jax.random.fold_in(jax.random.fold_in(own_key, 6), dim), (parts,), jnp.float32, least / len(cuts), largest / len(cuts))
        factor_of = factor_of * jnp.repeat(jnp.exp(heights), dims[dim] // parts).reshape((-1,) + (1,) * (len(dims) - 1 - dim))
    return factor_of


def scatter_about(own_key, dims, width, reach, shards=(), kind=jnp.bfloat16):
    entries = width * jax.random.normal(own_key, dims, jnp.float32)
    if shards:
        entries = entries * levels(own_key, dims, shards, -0.22, 0.18)
    return jnp.clip(entries, -reach, reach).astype(kind)


def setup_inputs(seed: int = 0) -> dict:
    seeds = jax.random.split(jax.random.key(seed), 9)
    forward_strain = scatter_about(seeds[0], (GROUPS, NDB, COMPS, NT), 1.0, 6.0, ((0, 4), (1, 32)))
    backward_strain = scatter_about(seeds[1], (GROUPS, NDB, COMPS, NT), 1.0, 6.0, ((0, 4), (1, 32)))
    request_point = with_ends(jax.random.randint(seeds[2], (OWNERS, OWNERS, CAP), 0, PDB_DEV), jax.random.fold_in(seeds[2], 1), 0, PDB_DEV - 1).astype(jnp.int32)
    node_slot = draw_node_slot(jax.random.fold_in(seeds[8], 71), 0)
    node_weight = jnp.clip(0.05 + 0.2 * jax.random.uniform(seeds[4], (2, K, POINTS), jnp.float32) ** levels(seeds[4], (2, K, POINTS), ((2, 32),), -0.2, 0.2), 0.05, 0.25)
    band_filter = jnp.clip(jnp.exp(jax.random.uniform(seeds[5], (BANDS, NF), jnp.float32, math.log(0.1), math.log(1.0))), 0.1, 1.0)
    misfit = jnp.clip(jnp.exp(jax.random.uniform(seeds[6], (STATION_PAIRS, BANDS), jnp.float32, math.log(0.1), math.log(1.0))), 0.1, 1.0)
    pair_group = draw_pair_group(jax.random.fold_in(seeds[8], 71), 0)
    return dict(forward_strain=forward_strain, backward_strain=backward_strain, request_point=request_point, node_slot=node_slot, node_weight=node_weight, band_filter=band_filter, misfit=misfit, pair_group=pair_group)


component_scale = (1.0, 1.0, 1.0, 2.0, 2.0, 2.0)


def make_table(time_steps, frequencies):
    time_index = lax.broadcasted_iota(jnp.int32, (time_steps, frequencies), 0)
    freq_index = lax.broadcasted_iota(jnp.int32, (time_steps, frequencies), 1)
    phase_angle = ((time_index * freq_index) % time_steps).astype(jnp.float32) * (2.0 * math.pi / time_steps)
    return jnp.concatenate([jnp.cos(phase_angle), -jnp.sin(phase_angle)], axis=1).astype(jnp.bfloat16)


def spectra(series, transform_table, rescale):
    series_rows = series.reshape(-1, series.shape[-1])
    projected = jnp.dot(series_rows, transform_table, preferred_element_type=jnp.float32) * rescale
    return projected.astype(jnp.bfloat16)


def combine_nodes(gathered, weight_block):
    weight_shape = weight_block.shape + (1,) * (gathered.ndim - 2)
    return jnp.sum(gathered.astype(jnp.float32) * weight_block.reshape(weight_shape), axis=0)


def mix_nodes(gathered_fwd, gathered_bwd, weight_fwd, weight_bwd):
    trailing = gathered_fwd.shape[3:]
    count = gathered_fwd.shape[1]
    mixed_fwd = combine_nodes(gathered_fwd, weight_fwd).reshape((count, 6, 2) + trailing)
    mixed_bwd = combine_nodes(gathered_bwd, weight_bwd).reshape((count, 6, 2) + trailing)
    products = mixed_fwd * mixed_bwd
    scale_shape = (1, 6, 1) + (1,) * len(trailing)
    weighted = products * jnp.array(component_scale, jnp.float32).reshape(scale_shape)
    return jnp.sum(weighted, axis=(1, 2))


def reference(forward_strain, backward_strain, request_point, node_slot, node_weight, band_filter, misfit, pair_group):
    transform_table = make_table(NT, NF)
    rescale = NT ** -0.5
    onehot = (pair_group[None, :] == jnp.arange(GROUPS, dtype=jnp.int32)[:, None]).astype(jnp.float32)
    group_weight = jnp.dot(onehot, misfit, precision=lax.Precision.HIGHEST)
    block_size = 64
    block_starts = jnp.arange(POINTS // block_size, dtype=jnp.int32) * block_size

    def group_term(group_index):
        forward = spectra(forward_strain[group_index], transform_table, rescale).reshape(NDB, 12, NF)
        backward = spectra(backward_strain[group_index], transform_table, rescale).reshape(NDB, 12, NF)

        def block_cross(start):
            owner_index = ((start + jnp.arange(block_size, dtype=jnp.int32)) // POINTS_DEV)[None, :]

            def fetch(table, which):
                slot_block = lax.dynamic_slice_in_dim(node_slot[which], start, block_size, 1)
                source = slot_block // CAP
                position = slot_block % CAP
                local_point = request_point[source, owner_index, position]
                return jnp.take(table, (source * PDB_DEV + local_point).astype(jnp.int32), axis=0)

            weight_fwd = lax.dynamic_slice_in_dim(node_weight[0], start, block_size, 1)
            weight_bwd = lax.dynamic_slice_in_dim(node_weight[1], start, block_size, 1)
            return mix_nodes(fetch(forward, 0), fetch(backward, 1), weight_fwd, weight_bwd)

        cross_spectra = lax.map(block_cross, block_starts).reshape(POINTS, NF)
        banded = jnp.einsum("bf,pf->bp", band_filter, cross_spectra, precision=lax.Precision.HIGHEST) * (NF ** -0.5)
        return banded * group_weight[group_index][:, None]

    terms = lax.map(group_term, jnp.arange(GROUPS, dtype=jnp.int32))
    return jnp.sum(terms, axis=0)
```

```python
import functools
import math

import jax
import jax.numpy as jnp
import ml_dtypes
import numpy as np
from jax import lax
from jax.experimental import pallas as pl
from jax.experimental.pallas import tpu as pltpu
from jax.sharding import PartitionSpec as P

MESH = pl.DeviceIdType.MESH
f32, bf16, i32 = jnp.float32, jnp.bfloat16, jnp.int32

SIDE = 4
CHIPS = SIDE * SIDE
PARTS = 3
BAND_SUM_TYPE = bf16


def table(steps, freqs, total):
    turn = (np.arange(steps)[:, None] * freqs[None, :] % total).astype(np.float32)
    angle = turn * np.float32(2.0 * math.pi / total)
    blocks = (len(freqs) // 32, 32)
    cos = np.cos(angle).reshape((steps,) + blocks)
    sin = -np.sin(angle).reshape((steps,) + blocks)
    both = np.stack([cos, sin], axis=2)
    return both.reshape(steps, 2 * len(freqs)).astype(ml_dtypes.bfloat16)


def tables(steps, count):
    even = np.stack([table(steps // 4, np.arange(r, count, 4), steps) for r in (0, 2)])
    odd = table(steps // 2, np.arange(1, count, 2), steps)
    return even, odd


def body(
    fs, bs, even_hbm, odd_hbm, slot, weight, request, band, misfit, group, out,
    xin, even, odd, fold_even, fold_odd, snd, got, nodef, node, sib, onehot, mix, rows, cross,
    bandx, rss, rsr, ysn, yrc,
    x_sem, t_sem, nd_s, nd_r, a_s, a_r, f_s, f_r, sb_s, sb_r, rs_s, rs_r, y_s, y_r,
):
    y = lax.axis_index("pair")
    d = lax.axis_index("db")
    core = d % 2
    chip = d // 2
    cx, cz = chip // SIDE, chip % SIDE
    planes = 4

    def chip_to(i):
        j = (i + 1) % CHIPS
        return ((cx + j // SIDE) % SIDE) * SIDE + (cz + j % SIDE) % SIDE

    def chip_from(i):
        j = (i + 1) % CHIPS
        return ((cx + SIDE - j // SIDE) % SIDE) * SIDE + (cz + SIDE - j % SIDE) % SIDE

    sibling = (y, chip * 2 + 1 - core)

    def remote(src, dst, s, r, dev):
        return pltpu.make_async_remote_copy(
            src_ref=src, dst_ref=dst, send_sem=s, recv_sem=r, device_id=dev, device_id_type=MESH
        )

    barrier = pltpu.get_barrier_semaphore()

    @pl.loop(0, CHIPS - 1)
    def _(i):
        pl.semaphore_signal(barrier, inc=1, device_id=(y, chip_to(i) * 2 + core), device_id_type=MESH)

    pl.semaphore_signal(barrier, inc=1, device_id=sibling, device_id_type=MESH)
    for step in range(1, planes):
        pl.semaphore_signal(barrier, inc=1, device_id=((y + step) % planes, d), device_id_type=MESH)

    def strain_load(t, w, h):
        source = (fs, bs)[w]
        return pltpu.make_async_copy(source.at[t + 3 * h], xin.at[t, 2 * w + h], x_sem.at[t, 2 * w + h])

    even_load = pltpu.make_async_copy(even_hbm, even, t_sem.at[0])
    odd_load = pltpu.make_async_copy(odd_hbm, odd, t_sem.at[1])
    for w in (0, 1):
        for h in (0, 1):
            strain_load(0, w, h).start()
    even_load.start()
    odd_load.start()
    for t in range(1, PARTS):
        for w in (0, 1):
            for h in (0, 1):
                strain_load(t, w, h).start()

    points = slot.shape[2]
    nodef[...] = jnp.zeros_like(nodef)
    for w in (0, 1):
        slots = slot[w]
        weights = weight[w]
        place = slots % 8
        which = lax.broadcasted_iota(i32, (8, points), 0)
        by_slot = jnp.zeros((8, points), f32)
        for k in range(8):
            by_slot += jnp.where(which == place[k : k + 1], weights[k : k + 1], 0.0)
        nodef[8 * w : 8 * w + 8, 0:points] = by_slot
        source = (slots[0:1] // 8).astype(f32)
        for q in range(points // 128):
            nodef[4 * w + q : 4 * w + q + 1, points : points + 128] = source[:, 128 * q : 128 * q + 128]
    lane = lax.broadcasted_iota(i32, (8, 256), 1)
    spread = (lane % 8 == lax.broadcasted_iota(i32, (8, 256), 0)).astype(f32)
    spread_out = lax.dot_general(
        request[...].astype(f32), spread, (((0,), (0,)), ((), ())), preferred_element_type=f32
    )
    owner = lax.broadcasted_iota(i32, (32, 256), 0)
    lane = lax.broadcasted_iota(i32, (32, 256), 1)
    for k in (0, 1):
        keep = (owner == 2 * (lane // 16) + k) & ((lane // 8) % 2 == core)
        row = jnp.sum(jnp.where(keep, spread_out, 0.0), axis=0, keepdims=True)
        for q in (0, 1):
            nodef[8 + 2 * k + q : 9 + 2 * k + q, points : points + 128] = row[:, 128 * q : 128 * q + 128]
    node[chip] = nodef[...].astype(bf16)

    pl.semaphore_wait(barrier, CHIPS - 1 + 1 + planes - 1)

    def node_copy(i):
        return remote(node.at[chip], node.at[chip], nd_s.at[i], nd_r.at[i], (y, chip_to(i) * 2 + core))

    @pl.loop(0, CHIPS - 1)
    def _(i):
        node_copy(i).start()

    local = xin.shape[2]
    steps = xin.shape[3]
    quarter = steps // 4
    rescale = steps ** (-0.5)
    width = 256

    def part_copy(t, i):
        to = chip_to(i)
        return remote(snd.at[t, to], got.at[t, chip, core], a_s.at[t, i], a_r.at[t, i], (y, to * 2 + core))

    def part_forward(t, i):
        s = chip_from(i)
        return remote(got.at[t, s, core], got.at[t, s, core], f_s.at[t, i], f_r.at[t, i], sibling)

    @pl.loop(0, PARTS)
    def _(t):
        for w in (0, 1):
            for h in (0, 1):
                slab = 2 * w + h
                pltpu.make_async_copy(fs.at[0], xin.at[t, slab], x_sem.at[t, slab]).wait()

                @pl.loop(0, quarter // width)
                def _(n):
                    at = pl.multiple_of(n * width, width)
                    x0, x1, x2, x3 = (
                        xin[t, slab, :, pl.ds(at + q * quarter, width)].astype(f32) for q in range(4)
                    )
                    a, b = x0 + x2, x1 + x3
                    span = pl.ds(slab * local, local)
                    fold_even[0, span, pl.ds(at, width)] = (a + b).astype(bf16)
                    fold_even[1, span, pl.ds(at, width)] = (a - b).astype(bf16)
                    fold_odd[span, pl.ds(at, width)] = (x0 - x2).astype(bf16)
                    fold_odd[span, pl.ds(at + quarter, width)] = (x1 - x3).astype(bf16)

        @pl.when(t == 0)
        def _():
            even_load.wait()
            odd_load.wait()

        for n in range(4):
            if n < 2:
                sums = jnp.dot(fold_even[n], even[n], preferred_element_type=f32)
            else:
                sums = jnp.dot(fold_odd[...], odd[:, (n - 2) * 256 : (n - 1) * 256], preferred_element_type=f32)
            sums = sums * rescale
            lanes = lax.broadcasted_iota(i32, (local, 128), 1)
            for u in (0, 1):
                for w in (0, 1):
                    first = sums[2 * w * local : (2 * w + 1) * local, 128 * u : 128 * u + 128]
                    second = sums[(2 * w + 1) * local : (2 * w + 2) * local, 128 * u : 128 * u + 128]
                    left = jnp.where(lanes < 64, first, pltpu.roll(second, 64, 1))
                    right = jnp.where(lanes < 64, pltpu.roll(first, 64, 1), second)
                    snd[t, 4 * n + 2 * u, :, 128 * w : 128 * w + 128] = left.astype(bf16)
                    snd[t, 4 * n + 2 * u + 1, :, 128 * w : 128 * w + 128] = right.astype(bf16)

        @pl.loop(0, CHIPS - 1)
        def _(i):
            part_copy(t, i).start()

        got[t, chip, core] = snd[t, chip]
        part_forward(t, CHIPS - 1).start()

    def receive(t):
        @pl.loop(0, CHIPS - 1)
        def _(i):
            part_copy(t, i).wait_recv()
            part_forward(t, i).start()

    receive(0)

    @pl.loop(0, CHIPS - 1)
    def _(i):
        node_copy(i).wait_recv()

    sib_copy = remote(node.at[:, :, pl.ds(points, 128)], sib, sb_s.at[0], sb_r.at[0], sibling)
    sib_copy.start()

    @pl.loop(0, CHIPS)
    def _(o):
        for w in (0, 1):
            for q in range(points // 128):
                by_slot = node[o, :, 128 * q : 128 * q + 128].astype(f32)[8 * w : 8 * w + 8]
                source = node[o, :, points : points + 128].astype(f32)[4 * w + q : 4 * w + q + 1]
                full = [jnp.where(source == float(e), by_slot, 0.0) for e in range(2 * CHIPS)]
                mix[o, w, 128 * q : 128 * q + 128, :] = jnp.concatenate(full, axis=0).T.astype(bf16)

    receive(1)
    sib_copy.wait_recv()

    @pl.loop(0, CHIPS)
    def _(s):
        mine = node[s, :, points : points + 128].astype(f32)
        theirs = sib[s].astype(f32)
        for q in (0, 1):
            mine_row = jnp.where(core == 0, mine[8 + q : 9 + q], mine[10 + q : 11 + q])
            their_row = jnp.where(core == 0, theirs[8 + q : 9 + q], theirs[10 + q : 11 + q])
            lane = lax.broadcasted_iota(i32, (128, 128), 1)
            place = lax.broadcasted_iota(i32, (128, 128), 0).astype(f32)
            wanted = mine_row + their_row + 64.0 * ((lane // 8) % 2).astype(f32)
            hits = jnp.where(place == wanted, 1.0, 0.0)
            onehot[s, 128 * q : 128 * q + 128, :] = hits.T.astype(bf16)

    count = band.shape[1]
    freq = lax.broadcasted_iota(i32, (count, 128), 0)
    at = lax.broadcasted_iota(i32, (count, 128), 1) % 32
    even_freq = 4 * (32 * (chip % 4) + at) + 2 * (chip // 4)
    odd_freq = 2 * (32 * (chip % 8) + at) + 1
    pick = (freq == jnp.where(chip < 8, even_freq, odd_freq)).astype(f32)
    chosen = jnp.dot(band[...], pick, precision=lax.Precision.HIGHEST, preferred_element_type=f32)
    own_group = (group[...] == y).astype(f32)
    group_weight = jnp.sum(misfit[...] * own_group, axis=1, keepdims=True)
    lane = lax.broadcasted_iota(i32, chosen.shape, 1)
    chosen = chosen * group_weight * jnp.where(lane < 64, 1.0, 2.0) * count ** (-0.5)
    high = chosen.astype(bf16).astype(f32)
    low = chosen - high
    bandx[...] = jnp.concatenate(
        [jnp.concatenate([high, high], axis=1), jnp.concatenate([low, jnp.zeros_like(low)], axis=1)], axis=0
    ).astype(bf16)

    def forwarded(t):
        @pl.loop(0, CHIPS)
        def _(i):
            s = chip_from(i)
            remote(
                got.at[t, s, core], got.at[t, s, 1 - core], f_s.at[t, i], f_r.at[t, i], sibling
            ).wait_recv()

    def gather(t):
        @pl.loop(0, CHIPS)
        def _(s):
            found = got[t, s].reshape(2 * local, 256)
            taken = jnp.dot(onehot[s], found, preferred_element_type=f32)
            taken = taken.reshape(CHIPS, 16, 256).astype(bf16)
            at = pl.ds(pl.multiple_of(s * 16, 16), 16)
            rows[:, at, 128 * t : 128 * t + 128] = taken[:, :, 0:128]
            rows[:, at, 384 + 128 * t : 512 + 128 * t] = taken[:, :, 128:256]

    for t in (0, 1):
        forwarded(t)
        gather(t)

    @pl.loop(0, CHIPS)
    def _(o):
        fwd = jnp.dot(mix[o, 0], rows[o, :, 0:256], preferred_element_type=f32)
        bwd = jnp.dot(mix[o, 1], rows[o, :, 384:640], preferred_element_type=f32)
        product = fwd * bwd
        cross[o] = product[:, 0:128] + product[:, 128:256]

    receive(2)
    forwarded(2)
    gather(2)

    def sum_copy(i):
        to = chip_to(i)
        return remote(rss.at[to], rsr.at[chip], rs_s.at[i], rs_r.at[i], (y, to * 2 + core))

    @pl.loop(0, CHIPS)
    def _(i):
        o = chip_to(i)
        fwd = jnp.dot(mix[o, 0], rows[o, :, 256:384], preferred_element_type=f32)
        bwd = jnp.dot(mix[o, 1], rows[o, :, 640:768], preferred_element_type=f32)
        total = cross[o] + fwd * bwd
        high = total.astype(bf16)
        low = (total - high.astype(f32)).astype(bf16)
        both = jnp.concatenate([high, low], axis=1)
        banded = lax.dot_general(bandx[...], both, (((1,), (1,)), ((), ())), preferred_element_type=f32)
        term = (banded[0:16] + banded[16:32]).astype(rss.dtype)

        @pl.when(i < CHIPS - 1)
        def _():
            rss[o] = term
            sum_copy(i).start()

        @pl.when(i == CHIPS - 1)
        def _():
            rsr[chip] = term

    @pl.loop(0, CHIPS - 1)
    def _(i):
        sum_copy(i).wait_recv()

    summed = jnp.sum(rsr[...].astype(f32), axis=0)
    for p in range(planes):
        ysn[p, 0:4, :] = summed[4 * p : 4 * p + 4]

    def plane_copy(step):
        to = (y + step) % planes
        return remote(ysn.at[to], yrc.at[step], y_s.at[step], y_r.at[step], (to, d))

    for step in range(1, planes):
        plane_copy(step).start()
    result = ysn[y, 0:4, :]
    for step in range(1, planes):
        plane_copy(step).wait_recv()
        result = result + yrc[step, 0:4, :]
    out[...] = result

    for step in range(1, planes):
        plane_copy(step).wait_send()
    sib_copy.wait_send()

    @pl.loop(0, CHIPS - 1)
    def _(i):
        node_copy(i).wait_send()
        sum_copy(i).wait_send()
        for t in range(PARTS):
            part_copy(t, i).wait_send()

    @pl.loop(0, CHIPS)
    def _(i):
        for t in range(PARTS):
            part_forward(t, i).wait_send()


def per_device(even, odd, fwd, bwd, request, slot, weight, band, misfit, group):
    comps, local, steps = fwd.shape[2], fwd.shape[1], fwd.shape[3]
    points = slot.shape[2]
    bands, count = band.shape
    args = (
        jnp.transpose(fwd[0], (1, 0, 2)),
        jnp.transpose(bwd[0], (1, 0, 2)),
        even,
        odd,
        slot,
        weight,
        jnp.transpose(request[0], (1, 0)),
        band,
        jnp.transpose(misfit, (1, 0)),
        group[None, :],
    )
    vmem = pl.BlockSpec(memory_space=pltpu.VMEM)
    hbm = pl.BlockSpec(memory_space=pltpu.HBM)
    dma = pltpu.SemaphoreType.DMA
    return pl.pallas_call(
        body,
        out_shape=jax.ShapeDtypeStruct((bands // 4, points), f32),
        in_specs=[hbm] * 4 + [vmem] * 6,
        out_specs=vmem,
        scratch_shapes=[
            pltpu.VMEM((PARTS, 4, local, steps), bf16),
            pltpu.VMEM(even.shape, bf16),
            pltpu.VMEM(odd.shape, bf16),
            pltpu.VMEM((2, 4 * local, steps // 4), bf16),
            pltpu.VMEM((4 * local, steps // 2), bf16),
            pltpu.VMEM((PARTS, CHIPS, local, 256), bf16),
            pltpu.VMEM((PARTS, CHIPS, 2, local, 256), bf16),
            pltpu.VMEM((16, points + 128), f32),
            pltpu.VMEM((CHIPS, 16, points + 128), bf16),
            pltpu.VMEM((CHIPS, 16, 128), bf16),
            pltpu.VMEM((CHIPS, 256, 2 * local), bf16),
            pltpu.VMEM((CHIPS, 2, points, 256), bf16),
            pltpu.VMEM((CHIPS, 256, 768), bf16),
            pltpu.VMEM((CHIPS, points, 128), f32),
            pltpu.VMEM((2 * bands, 256), bf16),
            pltpu.VMEM((CHIPS, bands, points), BAND_SUM_TYPE),
            pltpu.VMEM((CHIPS, bands, points), BAND_SUM_TYPE),
            pltpu.VMEM((4, 8, points), f32),
            pltpu.VMEM((4, 8, points), f32),
            dma((PARTS, 4)),
            dma((2,)),
            dma((CHIPS,)),
            dma((CHIPS,)),
            dma((PARTS, CHIPS)),
            dma((PARTS, CHIPS)),
            dma((PARTS, CHIPS)),
            dma((PARTS, CHIPS)),
            dma((1,)),
            dma((1,)),
            dma((CHIPS,)),
            dma((CHIPS,)),
            dma((4,)),
            dma((4,)),
        ],
        compiler_params=pltpu.CompilerParams(
            collective_id=0, has_side_effects=True, vmem_limit_bytes=60 * 2**20
        ),
    )(*args)


def solution(mesh):
    even, odd = tables(8192, 512)
    in_specs = (
        P(),
        P(),
        P("pair", "db", None, None),
        P("pair", "db", None, None),
        P("db", None, None),
        P(None, None, "db"),
        P(None, None, "db"),
        P(),
        P(),
        P(),
    )
    inner = jax.shard_map(
        per_device, mesh=mesh, in_specs=in_specs, out_specs=P("pair", "db"), check_vma=False
    )
    return lambda *args: inner(jnp.asarray(even), jnp.asarray(odd), *args)
```

```python
import functools
import math

import jax
import jax.numpy as jnp
import ml_dtypes
import numpy as np
from jax import lax
from jax.experimental import pallas as pl
from jax.experimental.pallas import tpu as pltpu
from jax.sharding import PartitionSpec as P

MESH = pl.DeviceIdType.MESH
f32, bf16, i32 = jnp.float32, jnp.bfloat16, jnp.int32

SIDE = 4
CHIPS = SIDE * SIDE
PLANES = 4
LAG = 4


def table(steps, freqs, total):
    turn = (np.arange(steps)[:, None] * freqs[None, :] % total).astype(np.float32)
    angle = turn * np.float32(2.0 * math.pi / total)
    blocks = (len(freqs) // 64, 64)
    cos = np.cos(angle).reshape((steps,) + blocks)
    sin = -np.sin(angle).reshape((steps,) + blocks)
    both = np.stack([cos, sin], axis=2)
    return both.reshape(steps, 2 * len(freqs)).astype(ml_dtypes.bfloat16)


def tables(steps, count):
    even = np.stack([table(steps // 4, np.arange(r, count, 4), steps) for r in (0, 2)])
    odd = table(steps // 2, np.arange(1, count, 2), steps)
    return even, odd


def body(
    fs, bs, even_hbm, odd_hbm, slot, weight, request, band, misfit, group, out,
    xin, even, odd, fold_even, fold_odd, snd0, snd1, got0, got1, nodef, node, quads, sib, onehot, mix, rows, cross,
    bandx, rss, rsr,
    x_sem, t_sem, nd_s, nd_r, q_s, q_r, a_s, a_r, f_s, f_r, sb_s, sb_r, rs_s, rs_r, plane_sem,
):
    y = lax.axis_index("pair")
    d = lax.axis_index("db")
    core = d % 2
    chip = d // 2
    cx, cz = chip // SIDE, chip % SIDE
    snds, gots = (snd0, snd1), (got0, got1)

    def hop(a):
        return (2 + 3 * a + 3 * (a * (a - 1) // 2)) % SIDE

    def chip_to(i):
        return ((cx + hop(i // SIDE)) % SIDE) * SIDE + (cz + hop(i % SIDE)) % SIDE

    def chip_from(i):
        return ((cx + SIDE - hop(i // SIDE)) % SIDE) * SIDE + (cz + SIDE - hop(i % SIDE)) % SIDE

    sibling = (y, chip * 2 + 1 - core)

    def remote(src, dst, s, r, dev):
        return pltpu.make_async_remote_copy(
            src_ref=src, dst_ref=dst, send_sem=s, recv_sem=r, device_id=dev, device_id_type=MESH
        )

    def strain_load(slab):
        t, w, h = slab // 4, slab // 2 % 2, slab % 2
        return pltpu.make_async_copy((fs, bs)[w].at[t + 3 * h], xin.at[slab], x_sem.at[slab])

    even_load = pltpu.make_async_copy(even_hbm, even, t_sem.at[0])
    odd_load = pltpu.make_async_copy(odd_hbm, odd, t_sem.at[1])
    for slab in range(4):
        strain_load(slab).start()
    even_load.start()
    odd_load.start()
    for slab in range(4, 12):
        strain_load(slab).start()

    barrier = pltpu.get_barrier_semaphore()

    @pl.loop(0, CHIPS - 1)
    def _(i):
        pl.semaphore_signal(barrier, inc=1, device_id=(y, chip_to(i) * 2 + core), device_id_type=MESH)

    for step in range(1, PLANES):
        pl.semaphore_signal(barrier, inc=1, device_id=((y + step) % PLANES, d), device_id_type=MESH)
    pl.semaphore_signal(barrier, inc=1, device_id=sibling, device_id_type=MESH)

    points = slot.shape[2]
    nodef[...] = jnp.zeros_like(nodef)
    for w in (0, 1):
        slots = slot[w]
        weights = weight[w]
        place = slots % 8
        which = lax.broadcasted_iota(i32, (8, points), 0)
        by_slot = jnp.zeros((8, points), f32)
        for k in range(8):
            by_slot += jnp.where(which == place[k : k + 1], weights[k : k + 1], 0.0)
        source = (slots[0:1] // 8).astype(f32)
        for q in range(PLANES):
            span = slice(128 * q, 128 * q + 128)
            own = jnp.where(y == q, 1.0, 0.0)
            nodef[8 * w : 8 * w + 8, :] += by_slot[:, span] * own
            nodef[16 + 4 * w + q : 17 + 4 * w + q, :] = source[:, span]
    lane = lax.broadcasted_iota(i32, (8, 256), 1)
    spread = (lane % 8 == lax.broadcasted_iota(i32, (8, 256), 0)).astype(f32)
    spread_out = lax.dot_general(
        request[...].astype(f32), spread, (((0,), (0,)), ((), ())), preferred_element_type=f32
    )
    owner = lax.broadcasted_iota(i32, (32, 256), 0)
    lane = lax.broadcasted_iota(i32, (32, 256), 1)
    for k in (0, 1):
        keep = (owner == 2 * (lane // 16) + k) & ((lane // 8) % 2 == core)
        row = jnp.sum(jnp.where(keep, spread_out, 0.0), axis=0, keepdims=True)
        for q in (0, 1):
            nodef[24 + 2 * k + q : 25 + 2 * k + q, :] = row[:, 128 * q : 128 * q + 128]
    node[chip] = nodef[...].astype(bf16)

    def node_copy(i):
        return remote(node.at[chip], node.at[chip], nd_s, nd_r, (y, chip_to(i) * 2 + core))

    def quad_copy(step):
        return remote(node.at[:, 0:16], quads.at[y], q_s, q_r, ((y + step) % PLANES, d))

    local = xin.shape[1]
    steps = xin.shape[2]
    quarter = steps // 4
    rescale = steps ** (-0.5)
    width = 256

    def part_copy(part, i):
        to = chip_to(i)
        return remote(
            snds[part].at[to], gots[part].at[chip, core], a_s.at[part], a_r.at[part, i], (y, to * 2 + core)
        )

    def part_forward(part, i, of):
        s = chip_from(i)
        return remote(
            gots[part].at[s, core], gots[part].at[s, of], f_s.at[part], f_r.at[part, i], sibling
        )

    def spectra(t, part, place, pairs):
        @pl.loop(0, 4)
        def _(r):
            slab = 4 * t + r
            pltpu.make_async_copy(fs.at[0], xin.at[slab], x_sem.at[slab]).wait()

            @pl.loop(0, quarter // width)
            def _(n):
                at = pl.multiple_of(n * width, width)
                x0, x1, x2, x3 = (xin[slab, :, pl.ds(at + q * quarter, width)].astype(f32) for q in range(4))
                a, b = x0 + x2, x1 + x3
                span = pl.ds(r * local, local)
                fold_even[0, span, pl.ds(at, width)] = (a + b).astype(bf16)
                fold_even[1, span, pl.ds(at, width)] = (a - b).astype(bf16)
                fold_odd[span, pl.ds(at, width)] = (x0 - x2).astype(bf16)
                fold_odd[span, pl.ds(at + quarter, width)] = (x1 - x3).astype(bf16)

        if t == 0:
            even_load.wait()
            odd_load.wait()
        for n in range(4):
            if n < 2:
                sums = jnp.dot(fold_even[n], even[n], preferred_element_type=f32)
            else:
                sums = jnp.dot(fold_odd[...], odd[:, (n - 2) * 256 : (n - 1) * 256], preferred_element_type=f32)
            sums = (sums * rescale).astype(bf16)
            for u in (0, 1):
                for r in range(4):
                    at = 128 * ((r // 2) * pairs + place)
                    snds[part][4 * n + 2 * u + r % 2, :, at : at + 128] = sums[
                        r * local : (r + 1) * local, 128 * u : 128 * u + 128
                    ]

    def depart(part):
        @pl.loop(0, CHIPS - 1)
        def _(i):
            part_copy(part, i).start()

        gots[part][chip, core] = snds[part][chip]
        part_forward(part, CHIPS - 1, core).start()

    spectra(0, 0, 0, 2)
    spectra(1, 0, 1, 2)

    pl.semaphore_wait(barrier, CHIPS - 1 + 1 + PLANES - 1)

    for step in range(1, PLANES):
        pl.semaphore_signal(plane_sem, inc=1, device_id=((y + step) % PLANES, d), device_id_type=MESH)

    @pl.loop(0, CHIPS - 1)
    def _(i):
        node_copy(i).start()

    depart(0)
    spectra(2, 1, 0, 1)
    depart(1)

    remote(node.at[0:15], node.at[0:15], nd_s, nd_r, sibling).wait_recv()
    sib_copy = remote(node.at[:, 16:32], sib, sb_s, sb_r, sibling)
    sib_copy.start()
    for step in range(1, PLANES):
        quad_copy(step).start()
    quads[y] = node[:, 0:16]

    count = band.shape[1]
    freq = lax.broadcasted_iota(i32, (count, 128), 0)
    at = lax.broadcasted_iota(i32, (count, 128), 1) % 64
    block = chip // 2
    even_freq = 4 * (64 * (block % 2) + at) + 2 * (block // 2)
    odd_freq = 2 * (64 * (block % 4) + at) + 1
    pick = (freq == jnp.where(block < 4, even_freq, odd_freq)).astype(f32)
    chosen = jnp.dot(band[...], pick, precision=lax.Precision.HIGHEST, preferred_element_type=f32)
    own_group = (group[...] == y).astype(f32)
    group_weight = jnp.sum(misfit[...] * own_group, axis=1, keepdims=True)
    component_scale = jnp.where(chip % 2 == 0, 1.0, 2.0)
    chosen = chosen * group_weight * (component_scale * count ** (-0.5))
    high = chosen.astype(bf16).astype(f32)
    low = chosen - high
    bandx[...] = jnp.concatenate(
        [jnp.concatenate([high, high], axis=1), jnp.concatenate([low, jnp.zeros_like(low)], axis=1)], axis=0
    ).astype(bf16)

    sib_copy.wait_recv()

    @pl.loop(0, CHIPS)
    def _(s):
        mine = node[s, 16:32].astype(f32)
        theirs = sib[s].astype(f32)
        for q in (0, 1):
            mine_row = jnp.where(core == 0, mine[8 + q : 9 + q], mine[10 + q : 11 + q])
            their_row = jnp.where(core == 0, theirs[8 + q : 9 + q], theirs[10 + q : 11 + q])
            lane = lax.broadcasted_iota(i32, (128, 128), 1)
            place = lax.broadcasted_iota(i32, (128, 128), 0).astype(f32)
            wanted = mine_row + their_row + 64.0 * ((lane // 8) % 2).astype(f32)
            hits = jnp.where(place == wanted, 1.0, 0.0)
            onehot[s, 128 * q : 128 * q + 128, :] = hits.T.astype(bf16)

    remote(quads.at[0:3], quads.at[0:3], q_s, q_r, sibling).wait_recv()

    @pl.loop(0, CHIPS)
    def _(o):
        sources = node[o, 16:32].astype(f32)
        for q in range(PLANES):
            quad = quads[q, o].astype(f32)
            for w in (0, 1):
                by_slot = quad[8 * w : 8 * w + 8]
                source = sources[4 * w + q : 4 * w + q + 1]
                for e in range(CHIPS):
                    two = [jnp.where(source == float(2 * e + k), by_slot, 0.0) for k in (0, 1)]
                    mix[o, w, 16 * e : 16 * e + 16, 128 * q : 128 * q + 128] = jnp.concatenate(
                        two, axis=0
                    ).astype(bf16)

    def receive(part, i):
        part_copy(part, i).wait_recv()
        part_forward(part, i, core).start()

    def gather(part, i):
        s = chip_from(i)
        part_forward(part, i, 1 - core).wait_recv()
        at = pl.ds(pl.multiple_of(s * 16, 16), 16)
        lanes = gots[part].shape[3]
        for n in range(lanes // 256):
            found = gots[part][s, :, :, 256 * n : 256 * n + 256].reshape(2 * local, 256)
            taken = jnp.dot(onehot[s], found, preferred_element_type=f32)
            rows[:, at, 512 * part + 256 * n : 512 * part + 256 * n + 256] = (
                taken.reshape(CHIPS, 16, 256).astype(bf16)
            )

    @pl.loop(0, CHIPS - 1 + LAG)
    def _(i):
        @pl.when(i < CHIPS - 1)
        def _():
            receive(0, i)

        @pl.when(i >= LAG)
        def _():
            gather(0, i - LAG)

    gather(0, CHIPS - 1)

    over_slots = (((0,), (0,)), ((), ()))

    def mixed(o, w, lanes):
        return lax.dot_general(rows[o, :, lanes], mix[o, w], over_slots, preferred_element_type=f32)

    @pl.loop(0, CHIPS, step=2)
    def _(o):
        receive(1, o)

        @pl.when(o < CHIPS - 2)
        def _():
            receive(1, o + 1)

        for e in (0, 1):
            product = mixed(o + e, 0, slice(0, 256)) * mixed(o + e, 1, slice(256, 512))
            cross[o + e] = product[0:128] + product[128:256]

        @pl.when(o >= LAG)
        def _():
            gather(1, o - LAG)
            gather(1, o + 1 - LAG)

    @pl.loop(CHIPS - LAG, CHIPS)
    def _(i):
        gather(1, i)

    pl.semaphore_wait(plane_sem, PLANES - 1)

    def sum_copy(i, step):
        to = chip_to(i)
        p = (y + step) % PLANES
        return remote(rss.at[to * PLANES + p], rsr.at[i * PLANES + step], rs_s, rs_r, (p, to * 2 + core))

    @pl.loop(0, CHIPS, step=2)
    def _(first):
        for e in (0, 1):
            o = chip_to(first + e)
            total = cross[o] + mixed(o, 0, slice(512, 640)) * mixed(o, 1, slice(640, 768))
            high = total.astype(bf16)
            low = (total - high.astype(f32)).astype(bf16)
            banded = jnp.dot(bandx[...], jnp.concatenate([high, low], axis=0), preferred_element_type=f32)
            banded = banded[0:16] + banded[16:32]
            for p in range(PLANES):
                pieces = [banded[4 * p : 4 * p + 4, 128 * q : 128 * q + 128] for q in range(points // 128)]
                rss[o * PLANES + p] = jnp.concatenate(pieces, axis=0).astype(bf16)
        for e in (0, 1):
            for step in (2, 1, 3):
                sum_copy(first + e, step).start()
        sum_copy(first, 0).start()

        @pl.when(first < CHIPS - 2)
        def _():
            sum_copy(first + 1, 0).start()

    own = (CHIPS - 1) * PLANES
    rsr[own] = rss[chip * PLANES + y]
    remote(rss.at[0:63], rsr.at[0:63], rs_s, rs_r, sibling).wait_recv()

    summed = jnp.sum(rsr[...].astype(f32), axis=0)
    for q in range(points // 128):
        out[:, 128 * q : 128 * q + 128] = summed[4 * q : 4 * q + 4]

    sib_copy.wait_send()
    remote(node.at[0:15], node.at[0:15], nd_s, nd_r, sibling).wait_send()
    remote(quads.at[0:3], quads.at[0:3], q_s, q_r, sibling).wait_send()
    remote(rss.at[0:63], rsr.at[0:63], rs_s, rs_r, sibling).wait_send()
    for part in (0, 1):
        sent, came = snds[part], gots[part]
        remote(sent.at[0:15], sent.at[0:15], a_s.at[part], a_r.at[part, 0], sibling).wait_send()
        remote(came.at[:, core], came.at[:, core], f_s.at[part], f_r.at[part, 0], sibling).wait_send()


def per_device(even, odd, fwd, bwd, request, slot, weight, band, misfit, group):
    comps, local, steps = fwd.shape[2], fwd.shape[1], fwd.shape[3]
    points = slot.shape[2]
    bands, count = band.shape
    args = (
        jnp.transpose(fwd[0], (1, 0, 2)),
        jnp.transpose(bwd[0], (1, 0, 2)),
        even,
        odd,
        slot,
        weight,
        jnp.transpose(request[0], (1, 0)),
        band,
        jnp.transpose(misfit, (1, 0)),
        group[None, :],
    )
    vmem = pl.BlockSpec(memory_space=pltpu.VMEM)
    hbm = pl.BlockSpec(memory_space=pltpu.HBM)
    dma = pltpu.SemaphoreType.DMA
    return pl.pallas_call(
        body,
        out_shape=jax.ShapeDtypeStruct((bands // 4, points), f32),
        in_specs=[hbm] * 4 + [vmem] * 6,
        out_specs=vmem,
        scratch_shapes=[
            pltpu.VMEM((12, local, steps), bf16),
            pltpu.VMEM(even.shape, bf16),
            pltpu.VMEM(odd.shape, bf16),
            pltpu.VMEM((2, 4 * local, steps // 4), bf16),
            pltpu.VMEM((4 * local, steps // 2), bf16),
            pltpu.VMEM((CHIPS, local, 512), bf16),
            pltpu.VMEM((CHIPS, local, 256), bf16),
            pltpu.VMEM((CHIPS, 2, local, 512), bf16),
            pltpu.VMEM((CHIPS, 2, local, 256), bf16),
            pltpu.VMEM((32, 128), f32),
            pltpu.VMEM((CHIPS, 32, 128), bf16),
            pltpu.VMEM((PLANES, CHIPS, 16, 128), bf16),
            pltpu.VMEM((CHIPS, 16, 128), bf16),
            pltpu.VMEM((CHIPS, 256, 2 * local), bf16),
            pltpu.VMEM((CHIPS, 2, 256, points), bf16),
            pltpu.VMEM((CHIPS, 256, 768), bf16),
            pltpu.VMEM((CHIPS, 128, points), f32),
            pltpu.VMEM((2 * bands, 256), bf16),
            pltpu.VMEM((CHIPS * PLANES, 16, 128), bf16),
            pltpu.VMEM((CHIPS * PLANES, 16, 128), bf16),
            dma((12,)),
            dma((2,)),
            dma,
            dma,
            dma,
            dma,
            dma((2,)),
            dma((2, CHIPS)),
            dma((2,)),
            dma((2, CHIPS)),
            dma,
            dma,
            dma,
            dma,
            pltpu.SemaphoreType.REGULAR,
        ],
        compiler_params=pltpu.CompilerParams(
            collective_id=0, has_side_effects=True, vmem_limit_bytes=60 * 2**20
        ),
    )(*args)


def solution(mesh):
    even, odd = tables(8192, 512)
    in_specs = (
        P(),
        P(),
        P("pair", "db", None, None),
        P("pair", "db", None, None),
        P("db", None, None),
        P(None, None, "db"),
        P(None, None, "db"),
        P(),
        P(),
        P(),
    )
    inner = jax.shard_map(
        per_device, mesh=mesh, in_specs=in_specs, out_specs=P("pair", "db"), check_vma=False
    )
    return lambda *args: inner(jnp.asarray(even), jnp.asarray(odd), *args)
```

```python
import functools
import math

import jax
import jax.numpy as jnp
import ml_dtypes
import numpy as np
from jax import lax
from jax.experimental import pallas as pl
from jax.experimental.pallas import tpu as pltpu
from jax.sharding import PartitionSpec as P

MESH = pl.DeviceIdType.MESH
f32, bf16, i32 = jnp.float32, jnp.bfloat16, jnp.int32

SIDE = 4
CHIPS = SIDE * SIDE
PLANES = 4
PARTS = 3


def table(steps, freqs, total):
    turn = (np.arange(steps)[:, None] * freqs[None, :] % total).astype(np.float32)
    angle = turn * np.float32(2.0 * math.pi / total)
    blocks = (len(freqs) // 64, 64)
    cos = np.cos(angle).reshape((steps,) + blocks)
    sin = -np.sin(angle).reshape((steps,) + blocks)
    both = np.stack([cos, sin], axis=2)
    return both.reshape(steps, 2 * len(freqs)).astype(ml_dtypes.bfloat16)


def tables(steps, count):
    even = np.stack([table(steps // 4, np.arange(r, count, 4), steps) for r in (0, 2)])
    odd = table(steps // 2, np.arange(1, count, 2), steps)
    return even, odd


def body(
    fs, bs, even_hbm, odd_hbm, slot, weight, request, band, misfit, group, out,
    xin, even, odd, fold_even, fold_odd, snd, got, nodef, node, quads, sib, onehot, mix, rows, cross,
    bandx, rss, rsr,
    x_sem, t_sem, nd_s, nd_r, q_s, q_r, a_s, a_r, f_s, f_r, sb_s, sb_r, rs_s, rs_r, plane_sem,
):
    y = lax.axis_index("pair")
    d = lax.axis_index("db")
    core = d % 2
    chip = d // 2
    cx, cz = chip // SIDE, chip % SIDE

    def hop(a):
        return 2 + 3 * a + 3 * (a * (a - 1) // 2)

    def row_to(a):
        return lax.rem(cx + hop(a), SIDE) * SIDE

    def row_from(a):
        return lax.rem(cx + 9 * SIDE - hop(a), SIDE) * SIDE

    order = (2, 1, 3, 0)
    z_to = [lax.rem(cz + h, SIDE) for h in order]
    z_from = [lax.rem(cz + SIDE - h, SIDE) for h in order]

    def others(act):
        @pl.loop(0, SIDE)
        def _(a):
            for b in range(SIDE - 1):
                act(a, b)

            @pl.when(a < SIDE - 1)
            def _():
                act(a, SIDE - 1)

    sibling = (y, chip * 2 + 1 - core)

    def remote(src, dst, s, r, dev):
        return pltpu.make_async_remote_copy(
            src_ref=src, dst_ref=dst, send_sem=s, recv_sem=r, device_id=dev, device_id_type=MESH
        )

    def strain_load(slab):
        t, w, h = slab // 4, slab // 2 % 2, slab % 2
        return pltpu.make_async_copy((fs, bs)[w].at[t + 3 * h], xin.at[slab], x_sem.at[slab])

    even_load = pltpu.make_async_copy(even_hbm, even, t_sem.at[0])
    odd_load = pltpu.make_async_copy(odd_hbm, odd, t_sem.at[1])
    for slab in range(4):
        strain_load(slab).start()
    even_load.start()
    odd_load.start()

    barrier = pltpu.get_barrier_semaphore()

    others(
        lambda a, b: pl.semaphore_signal(
            barrier, inc=1, device_id=(y, (row_to(a) + z_to[b]) * 2 + core), device_id_type=MESH
        )
    )
    for step in range(1, PLANES):
        pl.semaphore_signal(barrier, inc=1, device_id=((y + step) % PLANES, d), device_id_type=MESH)
    pl.semaphore_signal(barrier, inc=1, device_id=sibling, device_id_type=MESH)

    def node_copy(a, b):
        return remote(node.at[chip], node.at[chip], nd_s, nd_r, (y, (row_to(a) + z_to[b]) * 2 + core))

    def quad_copy(step):
        return remote(node.at[:, 0:16], quads.at[y], q_s, q_r, ((y + step) % PLANES, d))

    local = xin.shape[1]
    steps = xin.shape[2]
    quarter = steps // 4
    rescale = steps ** (-0.5)
    width = 256

    def part_copy(part, a, b):
        to = row_to(a) + z_to[b]
        return remote(
            snd.at[part, to], got.at[part, chip, core], a_s.at[part], a_r.at[part, a, b], (y, to * 2 + core)
        )

    def part_forward(part, a, b, of):
        s = row_from(a) + z_from[b]
        return remote(got.at[part, s, core], got.at[part, s, of], f_s.at[part], f_r.at[part, a, b], sibling)

    def spectra(t):
        @pl.loop(0, 4)
        def _(r):
            slab = 4 * t + r
            pltpu.make_async_copy(fs.at[0], xin.at[slab], x_sem.at[slab]).wait()

            @pl.loop(0, quarter // width)
            def _(n):
                at = pl.multiple_of(n * width, width)
                x0, x1, x2, x3 = (xin[slab, :, pl.ds(at + q * quarter, width)].astype(f32) for q in range(4))
                a, b = x0 + x2, x1 + x3
                span = pl.ds(r * local, local)
                fold_even[0, span, pl.ds(at, width)] = (a + b).astype(bf16)
                fold_even[1, span, pl.ds(at, width)] = (a - b).astype(bf16)
                fold_odd[span, pl.ds(at, width)] = (x0 - x2).astype(bf16)
                fold_odd[span, pl.ds(at + quarter, width)] = (x1 - x3).astype(bf16)

        if t < PARTS - 1:
            for slab in range(4 * t + 4, 4 * t + 8):
                strain_load(slab).start()
        if t == 0:
            even_load.wait()
            odd_load.wait()
        for n in range(4):
            if n < 2:
                sums = jnp.dot(fold_even[n], even[n], preferred_element_type=f32)
            else:
                sums = jnp.dot(fold_odd[...], odd[:, (n - 2) * 256 : (n - 1) * 256], preferred_element_type=f32)
            sums = (sums * rescale).astype(bf16)
            for u in (0, 1):
                for r in range(4):
                    at = 128 * (r // 2)
                    snd[t, 4 * n + 2 * u + r % 2, :, at : at + 128] = sums[
                        r * local : (r + 1) * local, 128 * u : 128 * u + 128
                    ]

    def depart(part):
        others(lambda a, b: part_copy(part, a, b).start())
        got[part, chip, core] = snd[part, chip]
        part_forward(part, SIDE - 1, SIDE - 1, core).start()

    spectra(0)

    points = slot.shape[2]
    nodef[...] = jnp.zeros_like(nodef)
    for w in (0, 1):
        slots = slot[w]
        weights = weight[w]
        place = slots % 8
        which = lax.broadcasted_iota(i32, (8, points), 0)
        by_slot = jnp.zeros((8, points), f32)
        for k in range(8):
            by_slot += jnp.where(which == place[k : k + 1], weights[k : k + 1], 0.0)
        source = (slots[0:1] // 8).astype(f32)
        for q in range(PLANES):
            span = slice(128 * q, 128 * q + 128)
            own = jnp.where(y == q, 1.0, 0.0)
            nodef[8 * w : 8 * w + 8, :] += by_slot[:, span] * own
            nodef[16 + 4 * w + q : 17 + 4 * w + q, :] = source[:, span]
    lane = lax.broadcasted_iota(i32, (8, 256), 1)
    spread = (lane % 8 == lax.broadcasted_iota(i32, (8, 256), 0)).astype(f32)
    spread_out = lax.dot_general(
        request[...].astype(f32), spread, (((0,), (0,)), ((), ())), preferred_element_type=f32
    )
    owner = lax.broadcasted_iota(i32, (32, 256), 0)
    lane = lax.broadcasted_iota(i32, (32, 256), 1)
    for k in (0, 1):
        keep = (owner == 2 * (lane // 16) + k) & ((lane // 8) % 2 == core)
        row = jnp.sum(jnp.where(keep, spread_out, 0.0), axis=0, keepdims=True)
        for q in (0, 1):
            nodef[24 + 2 * k + q : 25 + 2 * k + q, :] = row[:, 128 * q : 128 * q + 128]
    node[chip] = nodef[...].astype(bf16)

    pl.semaphore_wait(barrier, CHIPS - 1 + 1 + PLANES - 1)

    for step in range(1, PLANES):
        pl.semaphore_signal(plane_sem, inc=1, device_id=((y + step) % PLANES, d), device_id_type=MESH)

    others(lambda a, b: node_copy(a, b).start())
    depart(0)
    spectra(1)
    depart(1)
    spectra(2)
    depart(2)

    remote(node.at[0:15], node.at[0:15], nd_s, nd_r, sibling).wait_recv()
    sib_copy = remote(node.at[:, 16:32], sib, sb_s, sb_r, sibling)
    sib_copy.start()
    for step in range(1, PLANES):
        quad_copy(step).start()
    quads[y] = node[:, 0:16]

    count = band.shape[1]
    freq = lax.broadcasted_iota(i32, (count, 128), 0)
    at = lax.broadcasted_iota(i32, (count, 128), 1) % 64
    block = chip // 2
    even_freq = 4 * (64 * (block % 2) + at) + 2 * (block // 2)
    odd_freq = 2 * (64 * (block % 4) + at) + 1
    pick = (freq == jnp.where(block < 4, even_freq, odd_freq)).astype(f32)
    chosen = jnp.dot(band[...], pick, precision=lax.Precision.HIGHEST, preferred_element_type=f32)
    own_group = (group[...] == y).astype(f32)
    group_weight = jnp.sum(misfit[...] * own_group, axis=1, keepdims=True)
    component_scale = jnp.where(chip % 2 == 0, 1.0, 2.0)
    chosen = chosen * group_weight * (component_scale * count ** (-0.5))
    high = chosen.astype(bf16).astype(f32)
    low = chosen - high
    bandx[...] = jnp.concatenate(
        [jnp.concatenate([high, high], axis=1), jnp.concatenate([low, jnp.zeros_like(low)], axis=1)], axis=0
    ).astype(bf16)

    sib_copy.wait_recv()

    @pl.loop(0, CHIPS)
    def _(s):
        mine = node[s, 16:32].astype(f32)
        theirs = sib[s].astype(f32)
        for q in (0, 1):
            mine_row = jnp.where(core == 0, mine[8 + q : 9 + q], mine[10 + q : 11 + q])
            their_row = jnp.where(core == 0, theirs[8 + q : 9 + q], theirs[10 + q : 11 + q])
            lane = lax.broadcasted_iota(i32, (128, 128), 1)
            place = lax.broadcasted_iota(i32, (128, 128), 0).astype(f32)
            wanted = mine_row + their_row + 64.0 * ((lane // 8) % 2).astype(f32)
            hits = jnp.where(place == wanted, 1.0, 0.0)
            onehot[s, 128 * q : 128 * q + 128, :] = hits.T.astype(bf16)

    def receive(part, a):
        def one(b):
            part_copy(part, a, b).wait_recv()
            part_forward(part, a, b, core).start()

        for b in range(SIDE - 1):
            one(b)

        @pl.when(a < SIDE - 1)
        def _():
            one(SIDE - 1)

    def gather(part, a):
        for b in range(SIDE):
            part_forward(part, a, b, 1 - core).wait_recv()
        for b in range(SIDE):
            s = row_from(a) + z_from[b]
            at = pl.ds(pl.multiple_of(s * 16, 16), 16)
            found = got[part, s].reshape(2 * local, 256)
            taken = jnp.dot(onehot[s], found, preferred_element_type=f32)
            rows[:, at, 256 * part : 256 * part + 256] = taken.reshape(CHIPS, 16, 256).astype(bf16)

    @pl.loop(0, SIDE + 1)
    def _(a):
        @pl.when(a < SIDE)
        def _():
            receive(0, a)

        @pl.when(a >= 1)
        def _():
            gather(0, a - 1)

    remote(quads.at[0:3], quads.at[0:3], q_s, q_r, sibling).wait_recv()

    @pl.loop(0, CHIPS)
    def _(o):
        sources = node[o, 16:32].astype(f32)
        for q in range(PLANES):
            quad = quads[q, o].astype(f32)
            for w in (0, 1):
                by_slot = quad[8 * w : 8 * w + 8]
                source = sources[4 * w + q : 4 * w + q + 1]
                for e in range(CHIPS):
                    two = [jnp.where(source == float(2 * e + k), by_slot, 0.0) for k in (0, 1)]
                    mix[o, w, 16 * e : 16 * e + 16, 128 * q : 128 * q + 128] = jnp.concatenate(
                        two, axis=0
                    ).astype(bf16)

    over_slots = (((0,), (0,)), ((), ()))

    def mixed(o, w, part):
        at = 256 * part + 128 * w
        return lax.dot_general(rows[o, :, at : at + 128], mix[o, w], over_slots, preferred_element_type=f32)

    for part in (0, 1):
        @pl.loop(0, SIDE)
        def _(a):
            receive(part + 1, a)
            for e in range(SIDE):
                o = SIDE * a + e
                product = mixed(o, 0, part) * mixed(o, 1, part)
                cross[o] = product if part == 0 else cross[o] + product

        @pl.loop(0, SIDE)
        def _(a):
            gather(part + 1, a)

    pl.semaphore_wait(plane_sem, PLANES - 1)

    def sum_copy(a, b, step):
        to = row_to(a) + z_to[b]
        p = (y + step) % PLANES
        at = (SIDE * a + b) * PLANES + step
        return remote(rss.at[to * PLANES + p], rsr.at[at], rs_s, rs_r, (p, to * 2 + core))

    @pl.loop(0, SIDE)
    def _(a):
        for pair in (0, 2):
            for b in (pair, pair + 1):
                o = row_to(a) + z_to[b]
                total = cross[o] + mixed(o, 0, 2) * mixed(o, 1, 2)
                high = total.astype(bf16)
                low = (total - high.astype(f32)).astype(bf16)
                banded = jnp.dot(bandx[...], jnp.concatenate([high, low], axis=0), preferred_element_type=f32)
                banded = banded[0:16] + banded[16:32]
                for p in range(PLANES):
                    pieces = [banded[4 * p : 4 * p + 4, 128 * q : 128 * q + 128] for q in range(points // 128)]
                    rss[o * PLANES + p] = jnp.concatenate(pieces, axis=0).astype(bf16)
            for b in (pair, pair + 1):
                for step in (2, 1, 3):
                    sum_copy(a, b, step).start()
            sum_copy(a, pair, 0).start()
            if pair == 0:
                sum_copy(a, 1, 0).start()
            else:

                @pl.when(a < SIDE - 1)
                def _():
                    sum_copy(a, 3, 0).start()

    own = (CHIPS - 1) * PLANES
    rsr[own] = rss[chip * PLANES + y]
    remote(rss.at[0:63], rsr.at[0:63], rs_s, rs_r, sibling).wait_recv()

    summed = jnp.sum(rsr[...].astype(f32), axis=0)
    for q in range(points // 128):
        out[:, 128 * q : 128 * q + 128] = summed[4 * q : 4 * q + 4]

    sib_copy.wait_send()
    remote(node.at[0:15], node.at[0:15], nd_s, nd_r, sibling).wait_send()
    remote(quads.at[0:3], quads.at[0:3], q_s, q_r, sibling).wait_send()
    remote(rss.at[0:63], rsr.at[0:63], rs_s, rs_r, sibling).wait_send()
    for part in range(PARTS):
        sent, came = snd.at[part, 0:15], got.at[part, :, core]
        remote(sent, sent, a_s.at[part], a_r.at[part, 0, 0], sibling).wait_send()
        remote(came, came, f_s.at[part], f_r.at[part, 0, 0], sibling).wait_send()


def per_device(even, odd, fwd, bwd, request, slot, weight, band, misfit, group):
    comps, local, steps = fwd.shape[2], fwd.shape[1], fwd.shape[3]
    points = slot.shape[2]
    bands, count = band.shape
    args = (
        jnp.transpose(fwd[0], (1, 0, 2)),
        jnp.transpose(bwd[0], (1, 0, 2)),
        even,
        odd,
        slot,
        weight,
        jnp.transpose(request[0], (1, 0)),
        band,
        jnp.transpose(misfit, (1, 0)),
        group[None, :],
    )
    vmem = pl.BlockSpec(memory_space=pltpu.VMEM)
    hbm = pl.BlockSpec(memory_space=pltpu.HBM)
    dma = pltpu.SemaphoreType.DMA
    return pl.pallas_call(
        body,
        out_shape=jax.ShapeDtypeStruct((bands // 4, points), f32),
        in_specs=[hbm] * 4 + [vmem] * 6,
        out_specs=vmem,
        scratch_shapes=[
            pltpu.VMEM((12, local, steps), bf16),
            pltpu.VMEM(even.shape, bf16),
            pltpu.VMEM(odd.shape, bf16),
            pltpu.VMEM((2, 4 * local, steps // 4), bf16),
            pltpu.VMEM((4 * local, steps // 2), bf16),
            pltpu.VMEM((PARTS, CHIPS, local, 256), bf16),
            pltpu.VMEM((PARTS, CHIPS, 2, local, 256), bf16),
            pltpu.VMEM((32, 128), f32),
            pltpu.VMEM((CHIPS, 32, 128), bf16),
            pltpu.VMEM((PLANES, CHIPS, 16, 128), bf16),
            pltpu.VMEM((CHIPS, 16, 128), bf16),
            pltpu.VMEM((CHIPS, 256, 2 * local), bf16),
            pltpu.VMEM((CHIPS, 2, 256, points), bf16),
            pltpu.VMEM((CHIPS, 256, 768), bf16),
            pltpu.VMEM((CHIPS, 128, points), f32),
            pltpu.VMEM((2 * bands, 256), bf16),
            pltpu.VMEM((CHIPS * PLANES, 16, 128), bf16),
            pltpu.VMEM((CHIPS * PLANES, 16, 128), bf16),
            dma((12,)),
            dma((2,)),
            dma,
            dma,
            dma,
            dma,
            dma((PARTS,)),
            dma((PARTS, SIDE, SIDE)),
            dma((PARTS,)),
            dma((PARTS, SIDE, SIDE)),
            dma,
            dma,
            dma,
            dma,
            pltpu.SemaphoreType.REGULAR,
        ],
        compiler_params=pltpu.CompilerParams(
            collective_id=0, has_side_effects=True, vmem_limit_bytes=60 * 2**20
        ),
    )(*args)


def solution(mesh):
    even, odd = tables(8192, 512)
    in_specs = (
        P(),
        P(),
        P("pair", "db", None, None),
        P("pair", "db", None, None),
        P("db", None, None),
        P(None, None, "db"),
        P(None, None, "db"),
        P(),
        P(),
        P(),
    )
    inner = jax.shard_map(
        per_device, mesh=mesh, in_specs=in_specs, out_specs=P("pair", "db"), check_vma=False
    )
    return lambda *args: inner(jnp.asarray(even), jnp.asarray(odd), *args)
```

```python
import functools
import math

import jax
import jax.numpy as jnp
import ml_dtypes
import numpy as np
from jax import lax
from jax.experimental import pallas as pl
from jax.experimental.pallas import tpu as pltpu
from jax.sharding import PartitionSpec as P

MESH = pl.DeviceIdType.MESH
f32, bf16, i32 = jnp.float32, jnp.bfloat16, jnp.int32

SIDE = 4
CHIPS = SIDE * SIDE
PLANES = 4
PARTS = 3


def table(steps, freqs, total):
    turn = (np.arange(steps)[:, None] * freqs[None, :] % total).astype(np.float32)
    angle = turn * np.float32(2.0 * math.pi / total)
    blocks = (len(freqs) // 64, 64)
    cos = np.cos(angle).reshape((steps,) + blocks)
    sin = -np.sin(angle).reshape((steps,) + blocks)
    both = np.stack([cos, sin], axis=2)
    return both.reshape(steps, 2 * len(freqs)).astype(ml_dtypes.bfloat16)


def tables(steps, count):
    even = np.stack([table(steps // 4, np.arange(r, count, 4), steps) for r in (0, 2)])
    odd = table(steps // 2, np.arange(1, count, 2), steps)
    return even, odd


def body(
    fs, bs, even_hbm, odd_hbm, slot, weight, request, band, misfit, group, out,
    xin, even, odd, fold_even, fold_odd, snd, got, nodef, node, quads, sib, onehot, mix, rows, cross,
    bandx, rss, rsr,
    x_sem, t_sem, nd_s, nd_r, q_s, q_r, a_s, a_r, f_s, f_r, sb_s, sb_r, rs_s, rs_r, plane_sem,
):
    y = lax.axis_index("pair")
    d = lax.axis_index("db")
    core = d % 2
    chip = d // 2
    cx, cz = chip // SIDE, chip % SIDE

    def hop(a):
        return 2 + 3 * a + 3 * (a * (a - 1) // 2)

    def row_to(a):
        return lax.rem(cx + hop(a), SIDE) * SIDE

    def row_from(a):
        return lax.rem(cx + 9 * SIDE - hop(a), SIDE) * SIDE

    order = (2, 1, 3, 0)
    z_to = [lax.rem(cz + h, SIDE) for h in order]
    z_from = [lax.rem(cz + SIDE - h, SIDE) for h in order]
    z_db = [z * 2 + core for z in z_to]
    plane = [lax.rem(y + step, PLANES) for step in range(PLANES)]

    def others(act):
        @pl.loop(0, SIDE)
        def _(a):
            for b in range(SIDE - 1):
                act(a, b)

            @pl.when(a < SIDE - 1)
            def _():
                act(a, SIDE - 1)

    sibling = (y, chip * 2 + 1 - core)

    def remote(src, dst, s, r, dev):
        return pltpu.make_async_remote_copy(
            src_ref=src, dst_ref=dst, send_sem=s, recv_sem=r, device_id=dev, device_id_type=MESH
        )

    def strain_load(slab):
        t, w, h = slab // 4, slab // 2 % 2, slab % 2
        return pltpu.make_async_copy((fs, bs)[w].at[t + 3 * h], xin.at[slab], x_sem.at[slab])

    even_load = pltpu.make_async_copy(even_hbm, even, t_sem.at[0])
    odd_load = pltpu.make_async_copy(odd_hbm, odd, t_sem.at[1])
    for slab in range(4):
        strain_load(slab).start()

    even_load.start()
    odd_load.start()

    barrier = pltpu.get_barrier_semaphore()

    others(
        lambda a, b: pl.semaphore_signal(
            barrier, inc=1, device_id=(y, row_to(a) * 2 + z_db[b]), device_id_type=MESH
        )
    )
    for step in range(1, PLANES):
        pl.semaphore_signal(barrier, inc=1, device_id=((y + step) % PLANES, d), device_id_type=MESH)
    pl.semaphore_signal(barrier, inc=1, device_id=sibling, device_id_type=MESH)

    points = slot.shape[2]
    nodef[...] = jnp.zeros_like(nodef)
    for w in (0, 1):
        slots = slot[w]
        weights = weight[w]
        place = slots % 8
        which = lax.broadcasted_iota(i32, (8, points), 0)
        by_slot = jnp.zeros((8, points), f32)
        for k in range(8):
            by_slot += jnp.where(which == place[k : k + 1], weights[k : k + 1], 0.0)
        source = (slots[0:1] // 8).astype(f32)
        for q in range(PLANES):
            span = slice(128 * q, 128 * q + 128)
            own = jnp.where(y == q, 1.0, 0.0)
            nodef[8 * w : 8 * w + 8, :] += by_slot[:, span] * own
            nodef[16 + 4 * w + q : 17 + 4 * w + q, :] = source[:, span]
    lane = lax.broadcasted_iota(i32, (8, 256), 1)
    spread = (lane % 8 == lax.broadcasted_iota(i32, (8, 256), 0)).astype(f32)
    spread_out = lax.dot_general(
        request[...].astype(f32), spread, (((0,), (0,)), ((), ())), preferred_element_type=f32
    )
    owner = lax.broadcasted_iota(i32, (32, 256), 0)
    lane = lax.broadcasted_iota(i32, (32, 256), 1)
    for k in (0, 1):
        keep = (owner == 2 * (lane // 16) + k) & ((lane // 8) % 2 == core)
        row = jnp.sum(jnp.where(keep, spread_out, 0.0), axis=0, keepdims=True)
        for q in (0, 1):
            nodef[24 + 2 * k + q : 25 + 2 * k + q, :] = row[:, 128 * q : 128 * q + 128]
    node[chip] = nodef[...].astype(bf16)

    def node_copy(a, b):
        return remote(node.at[chip], node.at[chip], nd_s, nd_r, (y, row_to(a) * 2 + z_db[b]))

    def quad_copy(step):
        return remote(node.at[:, 0:16], quads.at[y], q_s, q_r, ((y + step) % PLANES, d))

    local = xin.shape[1]
    steps = xin.shape[2]
    quarter = steps // 4
    rescale = steps ** (-0.5)
    width = 256

    def part_copy(part, a, b):
        row = row_to(a)
        return remote(
            snd.at[part, row + z_to[b]],
            got.at[part, chip, core],
            a_s.at[part],
            a_r.at[part, a],
            (y, row * 2 + z_db[b]),
        )

    def part_forward(part, a, of):
        row = pl.ds(row_from(a), SIDE)
        return remote(got.at[part, row, core], got.at[part, row, of], f_s.at[part], f_r.at[part, a], sibling)

    def spectra(t):
        @pl.loop(0, 4)
        def _(r):
            slab = 4 * t + r
            pltpu.make_async_copy(fs.at[0], xin.at[slab], x_sem.at[slab]).wait()

            @pl.loop(0, quarter // width)
            def _(n):
                at = pl.multiple_of(n * width, width)
                x0, x1, x2, x3 = (xin[slab, :, pl.ds(at + q * quarter, width)].astype(f32) for q in range(4))
                a, b = x0 + x2, x1 + x3
                span = pl.ds(r * local, local)
                fold_even[0, span, pl.ds(at, width)] = (a + b).astype(bf16)
                fold_even[1, span, pl.ds(at, width)] = (a - b).astype(bf16)
                fold_odd[span, pl.ds(at, width)] = (x0 - x2).astype(bf16)
                fold_odd[span, pl.ds(at + quarter, width)] = (x1 - x3).astype(bf16)

        if t < PARTS - 1:
            for slab in range(4 * t + 4, 4 * t + 8):
                strain_load(slab).start()
        if t == 0:
            even_load.wait()
            odd_load.wait()
        for n in range(4):
            if n < 2:
                sums = jnp.dot(fold_even[n], even[n], preferred_element_type=f32)
            else:
                sums = jnp.dot(fold_odd[...], odd[:, (n - 2) * 256 : (n - 1) * 256], preferred_element_type=f32)
            sums = (sums * rescale).astype(bf16)
            for u in (0, 1):
                for r in range(4):
                    at = 128 * (r // 2)
                    snd[t, 4 * n + 2 * u + r % 2, :, at : at + 128] = sums[
                        r * local : (r + 1) * local, 128 * u : 128 * u + 128
                    ]

    def depart(part):
        others(lambda a, b: part_copy(part, a, b).start())
        got[part, chip, core] = snd[part, chip]

    spectra(0)

    pl.semaphore_wait(barrier, CHIPS - 1 + 1 + PLANES - 1)

    for step in range(1, PLANES):
        pl.semaphore_signal(plane_sem, inc=1, device_id=((y + step) % PLANES, d), device_id_type=MESH)

    others(lambda a, b: node_copy(a, b).start())
    depart(0)
    spectra(1)
    depart(1)
    spectra(2)
    depart(2)

    remote(node.at[0:15], node.at[0:15], nd_s, nd_r, sibling).wait_recv()
    sib_copy = remote(node.at[:, 16:32], sib, sb_s, sb_r, sibling)
    sib_copy.start()
    for step in range(1, PLANES):
        quad_copy(step).start()
    quads[y] = node[:, 0:16]

    count = band.shape[1]
    freq = lax.broadcasted_iota(i32, (count, 128), 0)
    at = lax.broadcasted_iota(i32, (count, 128), 1) % 64
    block = chip // 2
    even_freq = 4 * (64 * (block % 2) + at) + 2 * (block // 2)
    odd_freq = 2 * (64 * (block % 4) + at) + 1
    pick = (freq == jnp.where(block < 4, even_freq, odd_freq)).astype(f32)
    chosen = jnp.dot(band[...], pick, precision=lax.Precision.HIGHEST, preferred_element_type=f32)
    own_group = (group[...] == y).astype(f32)
    group_weight = jnp.sum(misfit[...] * own_group, axis=1, keepdims=True)
    component_scale = jnp.where(chip % 2 == 0, 1.0, 2.0)
    chosen = chosen * group_weight * (component_scale * count ** (-0.5))
    high = chosen.astype(bf16).astype(f32)
    low = chosen - high
    lane = lax.broadcasted_iota(i32, chosen.shape, 1)
    bandx[...] = jnp.concatenate([high, jnp.where(lane < 64, low, 0.0)], axis=0).astype(bf16)

    sib_copy.wait_recv()

    @pl.loop(0, CHIPS)
    def _(s):
        mine = node[s, 16:32].astype(f32)
        theirs = sib[s].astype(f32)
        for q in (0, 1):
            mine_row = jnp.where(core == 0, mine[8 + q : 9 + q], mine[10 + q : 11 + q])
            their_row = jnp.where(core == 0, theirs[8 + q : 9 + q], theirs[10 + q : 11 + q])
            lane = lax.broadcasted_iota(i32, (128, 128), 1)
            place = lax.broadcasted_iota(i32, (128, 128), 0).astype(f32)
            wanted = mine_row + their_row + 64.0 * ((lane // 8) % 2).astype(f32)
            hits = jnp.where(place == wanted, 1.0, 0.0)
            onehot[s, 128 * q : 128 * q + 128, :] = hits.T.astype(bf16)

    def receive(part, a):
        def arrived(count):
            blocks = got.at[part, 0:count, core]
            remote(blocks, blocks, a_s.at[part], a_r.at[part, a], sibling).wait_recv()

        @pl.when(a < SIDE - 1)
        def _():
            arrived(SIDE)

        @pl.when(a == SIDE - 1)
        def _():
            arrived(SIDE - 1)

        part_forward(part, a, core).start()

    def gather(part, a):
        part_forward(part, a, 1 - core).wait_recv()
        for b in range(SIDE):
            s = row_from(a) + z_from[b]
            at = pl.ds(pl.multiple_of(s * 16, 16), 16)
            found = got[part, s].reshape(2 * local, 256)
            taken = jnp.dot(onehot[s], found, preferred_element_type=f32)
            rows[:, at, 256 * part : 256 * part + 256] = taken.reshape(CHIPS, 16, 256).astype(bf16)

    remote(quads.at[0:3], quads.at[0:3], q_s, q_r, sibling).wait_recv()

    @pl.loop(0, CHIPS)
    def _(o):
        sources = node[o, 16:32].astype(f32)
        for q in range(PLANES):
            quad = quads[q, o].astype(f32)
            for w in (0, 1):
                by_slot = quad[8 * w : 8 * w + 8]
                source = sources[4 * w + q : 4 * w + q + 1]
                for e in range(CHIPS):
                    two = [jnp.where(source == float(2 * e + k), by_slot, 0.0) for k in (0, 1)]
                    mix[o, w, 16 * e : 16 * e + 16, 128 * q : 128 * q + 128] = jnp.concatenate(
                        two, axis=0
                    ).astype(bf16)

    @pl.loop(0, SIDE + 1)
    def _(a):
        @pl.when(a < SIDE)
        def _():
            receive(0, a)

        @pl.when(a >= 1)
        def _():
            gather(0, a - 1)

    over_slots = (((0,), (0,)), ((), ()))

    def mixed(o, w, part):
        at = 256 * part + 128 * w
        return lax.dot_general(rows[o, :, at : at + 128], mix[o, w], over_slots, preferred_element_type=f32)

    def halves(product):
        return product[0:64] + product[64:128]

    for part in (0, 1):

        @pl.loop(0, SIDE)
        def _(a):
            receive(part + 1, a)
            for e in range(SIDE):
                o = SIDE * a + e
                product = halves(mixed(o, 0, part) * mixed(o, 1, part))
                cross[o] = product if part == 0 else cross[o] + product

        @pl.loop(0, SIDE)
        def _(a):
            gather(part + 1, a)

    pl.semaphore_wait(plane_sem, PLANES - 1)

    def sum_copy(a, b, step):
        at = (SIDE * a + b) * PLANES
        p = plane[step]
        return remote(rss.at[at + p], rsr.at[at + step], rs_s, rs_r, (p, row_to(a) * 2 + z_db[b]))

    def sums_two(a, pair):
        for b in (pair, pair + 1):
            o = row_to(a) + z_to[b]
            total = cross[o] + halves(mixed(o, 0, 2) * mixed(o, 1, 2))
            high = total.astype(bf16)
            low = (total - high.astype(f32)).astype(bf16)
            banded = jnp.dot(bandx[...], jnp.concatenate([high, low], axis=0), preferred_element_type=f32)
            banded = banded[0:16] + banded[16:32]
            for p in range(PLANES):
                pieces = [banded[4 * p : 4 * p + 4, 128 * q : 128 * q + 128] for q in range(points // 128)]
                rss[(SIDE * a + b) * PLANES + p] = jnp.concatenate(pieces, axis=0).astype(bf16)

    def send_two(a, pair):
        for b in (pair, pair + 1):
            for step in (2, 1, 3) if (a, b) == (SIDE - 1, SIDE - 1) else (2, 1, 3, 0):
                sum_copy(a, b, step).start()

    pairs = [(a, pair) for a in range(SIDE) for pair in (0, 2)]
    for n, (a, pair) in enumerate(pairs):
        sums_two(a, pair)
        send_two(a, pair)

    own = (CHIPS - 1) * PLANES
    rsr[own] = rss[own + y]
    remote(rss.at[0:63], rsr.at[0:63], rs_s, rs_r, sibling).wait_recv()

    summed = jnp.sum(rsr[...].astype(f32), axis=0)
    for q in range(points // 128):
        out[:, 128 * q : 128 * q + 128] = summed[4 * q : 4 * q + 4]

    sib_copy.wait_send()
    remote(node.at[0:15], node.at[0:15], nd_s, nd_r, sibling).wait_send()
    remote(quads.at[0:3], quads.at[0:3], q_s, q_r, sibling).wait_send()
    remote(rss.at[0:63], rsr.at[0:63], rs_s, rs_r, sibling).wait_send()
    for part in range(PARTS):
        sent, came = snd.at[part, 0:15], got.at[part, :, core]
        remote(sent, sent, a_s.at[part], a_r.at[part, 0], sibling).wait_send()
        remote(came, came, f_s.at[part], f_r.at[part, 0], sibling).wait_send()


def per_device(even, odd, fwd, bwd, request, slot, weight, band, misfit, group):
    comps, local, steps = fwd.shape[2], fwd.shape[1], fwd.shape[3]
    points = slot.shape[2]
    bands, count = band.shape
    args = (
        jnp.transpose(fwd[0], (1, 0, 2)),
        jnp.transpose(bwd[0], (1, 0, 2)),
        even,
        odd,
        slot,
        weight,
        jnp.transpose(request[0], (1, 0)),
        band,
        jnp.transpose(misfit, (1, 0)),
        group[None, :],
    )
    vmem = pl.BlockSpec(memory_space=pltpu.VMEM)
    hbm = pl.BlockSpec(memory_space=pltpu.HBM)
    dma = pltpu.SemaphoreType.DMA
    return pl.pallas_call(
        body,
        out_shape=jax.ShapeDtypeStruct((bands // 4, points), f32),
        in_specs=[hbm] * 4 + [vmem] * 6,
        out_specs=vmem,
        scratch_shapes=[
            pltpu.VMEM((12, local, steps), bf16),
            pltpu.VMEM(even.shape, bf16),
            pltpu.VMEM(odd.shape, bf16),
            pltpu.VMEM((2, 4 * local, steps // 4), bf16),
            pltpu.VMEM((4 * local, steps // 2), bf16),
            pltpu.VMEM((PARTS, CHIPS, local, 256), bf16),
            pltpu.VMEM((PARTS, CHIPS, 2, local, 256), bf16),
            pltpu.VMEM((32, 128), f32),
            pltpu.VMEM((CHIPS, 32, 128), bf16),
            pltpu.VMEM((PLANES, CHIPS, 16, 128), bf16),
            pltpu.VMEM((CHIPS, 16, 128), bf16),
            pltpu.VMEM((CHIPS, 256, 2 * local), bf16),
            pltpu.VMEM((CHIPS, 2, 256, points), bf16),
            pltpu.VMEM((CHIPS, 256, 768), bf16),
            pltpu.VMEM((CHIPS, 64, points), f32),
            pltpu.VMEM((2 * bands, 128), bf16),
            pltpu.VMEM((CHIPS * PLANES, 16, 128), bf16),
            pltpu.VMEM((CHIPS * PLANES, 16, 128), bf16),
            dma((12,)),
            dma((2,)),
            dma,
            dma,
            dma,
            dma,
            dma((PARTS,)),
            dma((PARTS, SIDE)),
            dma((PARTS,)),
            dma((PARTS, SIDE)),
            dma,
            dma,
            dma,
            dma,
            pltpu.SemaphoreType.REGULAR,
        ],
        compiler_params=pltpu.CompilerParams(
            collective_id=0, has_side_effects=True, vmem_limit_bytes=60 * 2**20
        ),
    )(*args)


def solution(mesh):
    even, odd = tables(8192, 512)
    in_specs = (
        P(),
        P(),
        P("pair", "db", None, None),
        P("pair", "db", None, None),
        P("db", None, None),
        P(None, None, "db"),
        P(None, None, "db"),
        P(),
        P(),
        P(),
    )
    inner = jax.shard_map(
        per_device, mesh=mesh, in_specs=in_specs, out_specs=P("pair", "db"), check_vma=False
    )
    return lambda *args: inner(jnp.asarray(even), jnp.asarray(odd), *args)
```

```python
import functools
import math

import jax
import jax.numpy as jnp
import ml_dtypes
import numpy as np
from jax import lax
from jax.experimental import pallas as pl
from jax.experimental.pallas import tpu as pltpu
from jax.sharding import PartitionSpec as P

MESH = pl.DeviceIdType.MESH
f32, bf16, i32 = jnp.float32, jnp.bfloat16, jnp.int32

SIDE = 4
CHIPS = SIDE * SIDE
PLANES = 4
PARTS = 3


def table(steps, freqs, total):
    turn = (np.arange(steps)[:, None] * freqs[None, :] % total).astype(np.float32)
    angle = turn * np.float32(2.0 * math.pi / total)
    blocks = (len(freqs) // 64, 64)
    cos = np.cos(angle).reshape((steps,) + blocks)
    sin = -np.sin(angle).reshape((steps,) + blocks)
    both = np.stack([cos, sin], axis=2)
    return both.reshape(steps, 2 * len(freqs)).astype(ml_dtypes.bfloat16)


def tables(steps, count):
    even = np.stack([table(steps // 4, np.arange(r, count, 4), steps) for r in (0, 2)])
    odd = table(steps // 2, np.arange(1, count, 2), steps)
    return even, odd


def body(
    fs, bs, even_hbm, odd_hbm, slot, weight, request, band, misfit, group, out,
    xin, even, odd, fold_even, fold_odd, snd, got, nodef, node, quads, sib, onehot, mix, rows, cross,
    bandx, rss, rsr,
    x_sem, t_sem, nd_s, nd_r, q_s, q_r, a_s, a_r, f_s, f_r, sb_s, sb_r, rs_s, rs_r, plane_sem,
):
    y = lax.axis_index("pair")
    d = lax.axis_index("db")
    core = d % 2
    chip = d // 2
    cx, cz = chip // SIDE, chip % SIDE

    def hop(a):
        return 2 + 3 * a + 3 * (a * (a - 1) // 2)

    def row_to(a):
        return lax.rem(cx + hop(a), SIDE) * SIDE

    def row_from(a):
        return lax.rem(cx + 9 * SIDE - hop(a), SIDE) * SIDE

    order = (2, 1, 3, 0)
    z_to = [lax.rem(cz + h, SIDE) for h in order]
    z_from = [lax.rem(cz + SIDE - h, SIDE) for h in order]
    z_db = [z * 2 + core for z in z_to]
    plane = [lax.rem(y + step, PLANES) for step in range(PLANES)]

    def others(act):
        @pl.loop(0, SIDE)
        def _(a):
            for b in range(SIDE - 1):
                act(a, b)

            @pl.when(a < SIDE - 1)
            def _():
                act(a, SIDE - 1)

    sibling = (y, chip * 2 + 1 - core)

    def remote(src, dst, s, r, dev):
        return pltpu.make_async_remote_copy(
            src_ref=src, dst_ref=dst, send_sem=s, recv_sem=r, device_id=dev, device_id_type=MESH
        )

    def strain_load(slab):
        t, w, h = slab // 4, slab // 2 % 2, slab % 2
        return pltpu.make_async_copy((fs, bs)[w].at[t + 3 * h], xin.at[slab], x_sem.at[slab])

    even_load = pltpu.make_async_copy(even_hbm, even, t_sem.at[0])
    odd_load = pltpu.make_async_copy(odd_hbm, odd, t_sem.at[1])
    for slab in range(4):
        strain_load(slab).start()

    even_load.start()
    odd_load.start()

    barrier = pltpu.get_barrier_semaphore()

    others(
        lambda a, b: pl.semaphore_signal(
            barrier, inc=1, device_id=(y, row_to(a) * 2 + z_db[b]), device_id_type=MESH
        )
    )
    for step in range(1, PLANES):
        pl.semaphore_signal(barrier, inc=1, device_id=((y + step) % PLANES, d), device_id_type=MESH)
    pl.semaphore_signal(barrier, inc=1, device_id=sibling, device_id_type=MESH)

    points = slot.shape[2]
    nodef[...] = jnp.zeros_like(nodef)
    for w in (0, 1):
        slots = slot[w]
        weights = weight[w]
        place = slots % 8
        which = lax.broadcasted_iota(i32, (8, points), 0)
        by_slot = jnp.zeros((8, points), f32)
        for k in range(8):
            by_slot += jnp.where(which == place[k : k + 1], weights[k : k + 1], 0.0)
        source = (slots[0:1] // 8).astype(f32)
        for q in range(PLANES):
            span = slice(128 * q, 128 * q + 128)
            own = jnp.where(y == q, 1.0, 0.0)
            nodef[8 * w : 8 * w + 8, :] += by_slot[:, span] * own
            nodef[16 + 4 * w + q : 17 + 4 * w + q, :] = source[:, span]
    lane = lax.broadcasted_iota(i32, (8, 256), 1)
    spread = (lane % 8 == lax.broadcasted_iota(i32, (8, 256), 0)).astype(f32)
    spread_out = lax.dot_general(
        request[...].astype(f32), spread, (((0,), (0,)), ((), ())), preferred_element_type=f32
    )
    owner = lax.broadcasted_iota(i32, (32, 256), 0)
    lane = lax.broadcasted_iota(i32, (32, 256), 1)
    for k in (0, 1):
        keep = (owner == 2 * (lane // 16) + k) & ((lane // 8) % 2 == core)
        row = jnp.sum(jnp.where(keep, spread_out, 0.0), axis=0, keepdims=True)
        for q in (0, 1):
            nodef[24 + 2 * k + q : 25 + 2 * k + q, :] = row[:, 128 * q : 128 * q + 128]
    node[chip] = nodef[...].astype(bf16)

    def node_copy(a, b):
        return remote(node.at[chip], node.at[chip], nd_s, nd_r, (y, row_to(a) * 2 + z_db[b]))

    def quad_copy(step):
        return remote(node.at[:, 0:16], quads.at[y], q_s, q_r, ((y + step) % PLANES, d))

    local = xin.shape[1]
    steps = xin.shape[2]
    quarter = steps // 4
    rescale = steps ** (-0.5)
    width = 256

    def part_copy(part, a, b):
        row = row_to(a)
        return remote(
            snd.at[part, row + z_to[b]],
            got.at[part, chip, core],
            a_s.at[part],
            a_r.at[part, a],
            (y, row * 2 + z_db[b]),
        )

    def part_forward(part, a, of):
        row = pl.ds(row_from(a), SIDE)
        return remote(got.at[part, row, core], got.at[part, row, of], f_s.at[part], f_r.at[part, a], sibling)

    def spectra(t):
        @pl.loop(0, 4)
        def _(r):
            slab = 4 * t + r
            pltpu.make_async_copy(fs.at[0], xin.at[slab], x_sem.at[slab]).wait()

            @pl.loop(0, quarter // width)
            def _(n):
                at = pl.multiple_of(n * width, width)
                x0, x1, x2, x3 = (xin[slab, :, pl.ds(at + q * quarter, width)].astype(f32) for q in range(4))
                a, b = x0 + x2, x1 + x3
                span = pl.ds(r * local, local)
                fold_even[0, span, pl.ds(at, width)] = (a + b).astype(bf16)
                fold_even[1, span, pl.ds(at, width)] = (a - b).astype(bf16)
                fold_odd[span, pl.ds(at, width)] = (x0 - x2).astype(bf16)
                fold_odd[span, pl.ds(at + quarter, width)] = (x1 - x3).astype(bf16)

        if t < PARTS - 1:
            for slab in range(4 * t + 4, 4 * t + 8):
                strain_load(slab).start()
        if t == 0:
            even_load.wait()
            odd_load.wait()
        for n in range(4):
            if n < 2:
                sums = jnp.dot(fold_even[n], even[n], preferred_element_type=f32)
            else:
                sums = jnp.dot(fold_odd[...], odd[:, (n - 2) * 256 : (n - 1) * 256], preferred_element_type=f32)
            sums = (sums * rescale).astype(bf16)
            for u in (0, 1):
                for r in range(4):
                    at = 128 * (r // 2)
                    snd[t, 4 * n + 2 * u + r % 2, :, at : at + 128] = sums[
                        r * local : (r + 1) * local, 128 * u : 128 * u + 128
                    ]

    def depart(part):
        others(lambda a, b: part_copy(part, a, b).start())
        got[part, chip, core] = snd[part, chip]

    spectra(0)

    pl.semaphore_wait(barrier, CHIPS - 1 + 1 + PLANES - 1)

    for step in range(1, PLANES):
        pl.semaphore_signal(plane_sem, inc=1, device_id=((y + step) % PLANES, d), device_id_type=MESH)

    others(lambda a, b: node_copy(a, b).start())
    depart(0)
    spectra(1)
    depart(1)
    spectra(2)
    depart(2)

    remote(node.at[0:15], node.at[0:15], nd_s, nd_r, sibling).wait_recv()
    sib_copy = remote(node.at[:, 16:32], sib, sb_s, sb_r, sibling)
    sib_copy.start()
    for step in range(1, PLANES):
        quad_copy(step).start()
    quads[y] = node[:, 0:16]

    count = band.shape[1]
    freq = lax.broadcasted_iota(i32, (count, 128), 0)
    at = lax.broadcasted_iota(i32, (count, 128), 1) % 64
    block = chip // 2
    even_freq = 4 * (64 * (block % 2) + at) + 2 * (block // 2)
    odd_freq = 2 * (64 * (block % 4) + at) + 1
    pick = (freq == jnp.where(block < 4, even_freq, odd_freq)).astype(f32)
    chosen = jnp.dot(band[...], pick, precision=lax.Precision.HIGHEST, preferred_element_type=f32)
    own_group = (group[...] == y).astype(f32)
    group_weight = jnp.sum(misfit[...] * own_group, axis=1, keepdims=True)
    component_scale = jnp.where(chip % 2 == 0, 1.0, 2.0)
    chosen = chosen * group_weight * (component_scale * count ** (-0.5))
    high = chosen.astype(bf16).astype(f32)
    low = chosen - high
    lane = lax.broadcasted_iota(i32, chosen.shape, 1)
    bandx[...] = jnp.concatenate([high, jnp.where(lane < 64, low, 0.0)], axis=0).astype(bf16)

    sib_copy.wait_recv()

    @pl.loop(0, CHIPS, unroll=4)
    def _(s):
        mine = node[s, 16:32].astype(f32)
        theirs = sib[s].astype(f32)
        for q in (0, 1):
            mine_row = jnp.where(core == 0, mine[8 + q : 9 + q], mine[10 + q : 11 + q])
            their_row = jnp.where(core == 0, theirs[8 + q : 9 + q], theirs[10 + q : 11 + q])
            lane = lax.broadcasted_iota(i32, (128, 128), 1)
            place = lax.broadcasted_iota(i32, (128, 128), 0).astype(f32)
            wanted = mine_row + their_row + 64.0 * ((lane // 8) % 2).astype(f32)
            hits = jnp.where(place == wanted, 1.0, 0.0)
            onehot[s, 128 * q : 128 * q + 128, :] = hits.T.astype(bf16)

    def receive(part, a):
        def arrived(count):
            blocks = got.at[part, 0:count, core]
            remote(blocks, blocks, a_s.at[part], a_r.at[part, a], sibling).wait_recv()

        @pl.when(a < SIDE - 1)
        def _():
            arrived(SIDE)

        @pl.when(a == SIDE - 1)
        def _():
            arrived(SIDE - 1)

        part_forward(part, a, core).start()

    def gather(part, a):
        part_forward(part, a, 1 - core).wait_recv()
        for b in range(SIDE):
            s = row_from(a) + z_from[b]
            at = pl.ds(pl.multiple_of(s * 16, 16), 16)
            found = got[part, s].reshape(2 * local, 256)
            taken = jnp.dot(onehot[s], found, preferred_element_type=f32)
            rows[:, at, 256 * part : 256 * part + 256] = taken.reshape(CHIPS, 16, 256).astype(bf16)

    remote(quads.at[0:3], quads.at[0:3], q_s, q_r, sibling).wait_recv()

    @pl.loop(0, CHIPS)
    def _(o):
        sources = node[o, 16:32].astype(f32)
        for q in range(PLANES):
            quad = quads[q, o].astype(f32)
            for w in (0, 1):
                by_slot = quad[8 * w : 8 * w + 8]
                source = sources[4 * w + q : 4 * w + q + 1]
                for e in range(CHIPS):
                    two = [jnp.where(source == float(2 * e + k), by_slot, 0.0) for k in (0, 1)]
                    mix[o, w, 16 * e : 16 * e + 16, 128 * q : 128 * q + 128] = jnp.concatenate(
                        two, axis=0
                    ).astype(bf16)

    @pl.loop(0, SIDE + 1)
    def _(a):
        @pl.when(a < SIDE)
        def _():
            receive(0, a)

        @pl.when(a >= 1)
        def _():
            gather(0, a - 1)

    over_slots = (((0,), (0,)), ((), ()))

    def mixed(o, w, part):
        at = 256 * part + 128 * w
        return lax.dot_general(rows[o, :, at : at + 128], mix[o, w], over_slots, preferred_element_type=f32)

    def halves(product):
        return product[0:64] + product[64:128]

    for part in (0, 1):

        @pl.loop(0, SIDE)
        def _(a):
            receive(part + 1, a)
            for e in range(SIDE):
                o = SIDE * a + e
                product = halves(mixed(o, 0, part) * mixed(o, 1, part))
                cross[o] = product if part == 0 else cross[o] + product

        @pl.loop(0, SIDE)
        def _(a):
            gather(part + 1, a)

    pl.semaphore_wait(plane_sem, PLANES - 1)

    def sum_copy(a, b, step):
        at = (SIDE * a + b) * PLANES
        p = plane[step]
        return remote(rss.at[at + p], rsr.at[at + step], rs_s, rs_r, (p, row_to(a) * 2 + z_db[b]))

    def sums_two(a, pair):
        for b in (pair, pair + 1):
            o = row_to(a) + z_to[b]
            total = cross[o] + halves(mixed(o, 0, 2) * mixed(o, 1, 2))
            high = total.astype(bf16)
            low = (total - high.astype(f32)).astype(bf16)
            banded = jnp.dot(bandx[...], jnp.concatenate([high, low], axis=0), preferred_element_type=f32)
            banded = banded[0:16] + banded[16:32]
            for p in range(PLANES):
                pieces = [banded[4 * p : 4 * p + 4, 128 * q : 128 * q + 128] for q in range(points // 128)]
                rss[(SIDE * a + b) * PLANES + p] = jnp.concatenate(pieces, axis=0).astype(bf16)

    def send_two(a, pair):
        for b in (pair, pair + 1):
            for step in (2, 1, 3) if (a, b) == (SIDE - 1, SIDE - 1) else (2, 1, 3, 0):
                sum_copy(a, b, step).start()

    pairs = [(a, pair) for a in range(SIDE) for pair in (0, 2)]
    for n, (a, pair) in enumerate(pairs):
        sums_two(a, pair)
        send_two(a, pair)

    own = (CHIPS - 1) * PLANES
    rsr[own] = rss[own + y]
    remote(rss.at[0:63], rsr.at[0:63], rs_s, rs_r, sibling).wait_recv()

    summed = jnp.sum(rsr[...].astype(f32), axis=0)
    for q in range(points // 128):
        out[:, 128 * q : 128 * q + 128] = summed[4 * q : 4 * q + 4]

    sib_copy.wait_send()
    remote(node.at[0:15], node.at[0:15], nd_s, nd_r, sibling).wait_send()
    remote(quads.at[0:3], quads.at[0:3], q_s, q_r, sibling).wait_send()
    remote(rss.at[0:63], rsr.at[0:63], rs_s, rs_r, sibling).wait_send()
    for part in range(PARTS):
        sent, came = snd.at[part, 0:15], got.at[part, :, core]
        remote(sent, sent, a_s.at[part], a_r.at[part, 0], sibling).wait_send()
        remote(came, came, f_s.at[part], f_r.at[part, 0], sibling).wait_send()


def per_device(even, odd, fwd, bwd, request, slot, weight, band, misfit, group):
    comps, local, steps = fwd.shape[2], fwd.shape[1], fwd.shape[3]
    points = slot.shape[2]
    bands, count = band.shape
    args = (
        jnp.transpose(fwd[0], (1, 0, 2)),
        jnp.transpose(bwd[0], (1, 0, 2)),
        even,
        odd,
        slot,
        weight,
        jnp.transpose(request[0], (1, 0)),
        band,
        jnp.transpose(misfit, (1, 0)),
        group[None, :],
    )
    vmem = pl.BlockSpec(memory_space=pltpu.VMEM)
    hbm = pl.BlockSpec(memory_space=pltpu.HBM)
    dma = pltpu.SemaphoreType.DMA
    return pl.pallas_call(
        body,
        out_shape=jax.ShapeDtypeStruct((bands // 4, points), f32),
        in_specs=[hbm] * 4 + [vmem] * 6,
        out_specs=vmem,
        scratch_shapes=[
            pltpu.VMEM((12, local, steps), bf16),
            pltpu.VMEM(even.shape, bf16),
            pltpu.VMEM(odd.shape, bf16),
            pltpu.VMEM((2, 4 * local, steps // 4), bf16),
            pltpu.VMEM((4 * local, steps // 2), bf16),
            pltpu.VMEM((PARTS, CHIPS, local, 256), bf16),
            pltpu.VMEM((PARTS, CHIPS, 2, local, 256), bf16),
            pltpu.VMEM((32, 128), f32),
            pltpu.VMEM((CHIPS, 32, 128), bf16),
            pltpu.VMEM((PLANES, CHIPS, 16, 128), bf16),
            pltpu.VMEM((CHIPS, 16, 128), bf16),
            pltpu.VMEM((CHIPS, 256, 2 * local), bf16),
            pltpu.VMEM((CHIPS, 2, 256, points), bf16),
            pltpu.VMEM((CHIPS, 256, 768), bf16),
            pltpu.VMEM((CHIPS, 64, points), f32),
            pltpu.VMEM((2 * bands, 128), bf16),
            pltpu.VMEM((CHIPS * PLANES, 16, 128), bf16),
            pltpu.VMEM((CHIPS * PLANES, 16, 128), bf16),
            dma((12,)),
            dma((2,)),
            dma,
            dma,
            dma,
            dma,
            dma((PARTS,)),
            dma((PARTS, SIDE)),
            dma((PARTS,)),
            dma((PARTS, SIDE)),
            dma,
            dma,
            dma,
            dma,
            pltpu.SemaphoreType.REGULAR,
        ],
        compiler_params=pltpu.CompilerParams(
            collective_id=0, has_side_effects=True, vmem_limit_bytes=60 * 2**20
        ),
    )(*args)


def solution(mesh):
    even, odd = tables(8192, 512)
    in_specs = (
        P(),
        P(),
        P("pair", "db", None, None),
        P("pair", "db", None, None),
        P("db", None, None),
        P(None, None, "db"),
        P(None, None, "db"),
        P(),
        P(),
        P(),
    )
    inner = jax.shard_map(
        per_device, mesh=mesh, in_specs=in_specs, out_specs=P("pair", "db"), check_vma=False
    )
    return lambda *args: inner(jnp.asarray(even), jnp.asarray(odd), *args)
```
